512 devices in a mesh: row: 16 (over z_lo, x), col: 8 (over y), fiber: 4 (over z_hi, core).
Axes of the slice: x: 4, y: 8, z: 8 (z_hi: 2, z_lo: 4; z = z_hi * 4 + z_lo), core: 2. Of those that a mesh axis runs over, the one named last changes fastest.
Arguments:
- values: float32 [12288, 12288], P('row', ('col', 'fiber')), may hold values from -6 to 6
- tile_mask: int32 [96, 96], P('row', ('col', 'fiber')), may hold values from 0 to 1, as said below
- keep_mask: int32 [96, 96], P('row', ('col', 'fiber')), may hold values 0 or 1
Outputs:
- flows: float32 [12288, 12288], P('row', ('col', 'fiber'))
The draws below stay inside these ranges and needn't reach their ends.
Inputs may be any that keep to these rules, and one draw needn't show every extreme that they name: `tile_mask`: 1 marks a tile that holds entries; every diagonal tile is 1, and tiles with low indices are denser.
All inputs are finite; a program needn't handle non-finite values. No bound on the sum of `keep_mask` on one device may be relied on, other than what follows from the above.
Results may differ from the reference program's by a relative error of at most 0.017.
Values may be sent and summed in bfloat16 or wider, within the bound.
No kernel may reach another device: no remote copies, remote signals or barrier semaphores. Data moves between devices by JAX's collectives and lax.ppermute only.
A program may use at most 64 MiB of HBM per device.

```python
import jax
import jax.numpy as jnp
from jax import lax

UNIT = 384
N = 12288
NTILES = 96
N_FIBER = 4


def draw_tile_mask(key, part):
    indices = jnp.arange(NTILES, dtype=jnp.int32)
    row_ids = indices[:, None]
    col_ids = indices[None, :]
    levels = max(1, (NTILES - 1).bit_length())
    agreement = jnp.zeros((NTILES, NTILES), jnp.int32)
    both_low = jnp.zeros((NTILES, NTILES), jnp.int32)
    for level in range(levels):
        row_bit = row_ids >> level & 1
        col_bit = col_ids >> level & 1
        agreement = agreement + (row_bit == col_bit).astype(jnp.int32)
        both_low = both_low + ((row_bit == 0) & (col_bit == 0)).astype(jnp.int32)
    ticket = jax.random.randint(jax.random.fold_in(key, 17), (NTILES, NTILES), 0, 2 * levels + 1)
    kept_tiles = (ticket <= agreement + both_low) | (row_ids == col_ids)
    return kept_tiles.astype(jnp.int32)


def place_ends(values, stream_key, smallest, largest):
    longest = values.shape.index(max(values.shape))
    spots = []
    for shift in (0, 1):
        where = [jax.random.randint(jax.random.fold_in(stream_key, axis), (), 0, length) for axis, length in enumerate(values.shape)]
        where[longest] = (where[longest] + shift) % values.shape[longest]
        spots.append(tuple(where))
    return values.at[spots[0]].set(smallest).at[spots[1]].set(largest)


def steps_of(stream_key, extent, cuts, low, top_value):
    gain, own = 1.0, jax.random.fold_in(stream_key, 6)
    for axis_at, parts in cuts:
        draws = jnp.exp(jax.random.uniform(jax.random.fold_in(own, axis_at), (parts,), jnp.float32, low / len(cuts), top_value / len(cuts)))
        gain = gain * jnp.repeat(draws, extent[axis_at] // parts).reshape([-1 if axis == axis_at else 1 for axis in range(len(extent))])
    return gain


def scatter_about(rng, dims, spread, most, split=(), held_as=jnp.bfloat16):
    level = steps_of(rng, dims, split, -0.22, 0.18) if split else 1.0
    result = jax.random.normal(rng, dims, jnp.float32) * spread * level
    return jnp.minimum(jnp.maximum(result, -most), most).astype(held_as)


def setup_inputs(seed: int = 0) -> dict:
    seeds = jax.random.split(jax.random.key(seed), 4)
    return {
        "values": scatter_about(seeds[0], (N, N), 1.0, 6.0, ((0, 16), (1, 32)), jnp.float32),
        "tile_mask": draw_tile_mask(jax.random.fold_in(seeds[3], 71), 0),
        "keep_mask": place_ends((jax.random.randint(seeds[2], (NTILES, NTILES), 0, 4) < 3).astype(jnp.int32), jax.random.fold_in(seeds[2], 1), 0, 1),
    }


def spread_tiles(mask, tile_size):
    count_rows, count_cols = mask.shape
    wide = jnp.broadcast_to(mask.astype(jnp.float32)[:, None, :, None], (count_rows, tile_size, count_cols, tile_size))
    return wide.reshape(count_rows * tile_size, count_cols * tile_size)


def reference(values, tile_mask, keep_mask):
    tile_size = values.shape[0] // tile_mask.shape[0]
    total = values.shape[0]
    sub_width = UNIT // N_FIBER
    weighted = (values * spread_tiles(tile_mask, tile_size)).astype(jnp.bfloat16)
    layer_cols = weighted.reshape(total, total // UNIT, N_FIBER, sub_width)
    layer_rows = weighted.reshape(total // UNIT, N_FIBER, sub_width, total)

    def add_layer(layer, running):
        left_part = lax.dynamic_index_in_dim(layer_cols, layer, 2, keepdims=False).reshape(total, (total // UNIT) * sub_width)
        right_part = lax.dynamic_index_in_dim(layer_rows, layer, 1, keepdims=False).reshape((total // UNIT) * sub_width, total)
        product = jnp.dot(left_part, right_part, preferred_element_type=jnp.float32)
        return running + product.astype(jnp.bfloat16).astype(jnp.float32)

    expanded = lax.fori_loop(0, N_FIBER, add_layer, jnp.zeros((total, total), jnp.float32))
    squared = expanded * expanded
    col_scale = jnp.mean(squared, axis=0) + 1e-6
    return spread_tiles(keep_mask, tile_size) * squared / col_scale[None, :]
```

```python
import jax
import jax.numpy as jnp
from jax import lax
from jax.sharding import Mesh
from jax.sharding import PartitionSpec as P

Z_LO, X, Y, Z_HI, CORE = 4, 4, 8, 2, 2
Z = Z_LO * Z_HI


def spread_tiles(mask, tile_size):
    count_rows, count_cols = mask.shape
    wide = jnp.broadcast_to(
        mask.astype(jnp.float32)[:, None, :, None], (count_rows, tile_size, count_cols, tile_size)
    )
    return wide.reshape(count_rows * tile_size, count_cols * tile_size)


def z_index(z):
    return (z % Z_LO) * Z_HI + z // Z_LO


def shift_z(shard, step):
    pairs = [(z_index(z), z_index((z + step) % Z)) for z in range(Z)]
    return lax.ppermute(shard, ("zlo", "zhi"), pairs)


def shift_x(shard, step):
    return lax.ppermute(shard, "x", [(i, (i + step) % X) for i in range(X)])


def swap(shard, axis):
    return lax.ppermute(shard, axis, [(0, 1), (1, 0)])


def pick(stack, index):
    return lax.dynamic_index_in_dim(stack, index, 0, keepdims=False)


def ring(shard):
    half = shard.shape[0] // 2
    arrived = [(0, shard)]
    up = down = shard
    for d in range(1, Z // 2):
        up, down = shift_z(up, 1), shift_z(down, -1)
        arrived += [(d, up), (-d, down)]
    far = jnp.concatenate([shift_z(up[:half], 1), shift_z(down[half:], -1)], 0)
    return arrived + [(Z // 2, far)]


def local(values, tile_mask, keep_mask):
    rows, unit = values.shape
    tile_size = unit // tile_mask.shape[1]
    sub = unit // (X * CORE)
    half = rows // 2
    x, core, zhi, zlo = (lax.axis_index(a) for a in ("x", "core", "zhi", "zlo"))
    z = zhi * Z_LO + zlo
    weighted = (values * spread_tiles(tile_mask, tile_size)).astype(jnp.bfloat16)

    left = weighted.T.reshape(X * CORE, sub, 2, half).transpose(0, 2, 1, 3)
    right = weighted.reshape(CORE, X * CORE, sub, unit).transpose(1, 0, 2, 3)
    both = jnp.concatenate([left, right], 1)
    both = lax.all_to_all(both, ("x", "core"), split_axis=0, concat_axis=0, tiled=True)
    both = both.reshape(X, CORE, 4, sub, unit)

    left = both[:, :, :2].transpose(2, 1, 3, 0, 4).reshape(2, CORE * sub, X * half)
    left_near = pick(left, zhi)
    left_far = swap(pick(left, 1 - zhi), "zhi")
    left_near = lax.all_gather(left_near, "y", axis=0, tiled=True)
    left_far = lax.all_gather(left_far, "y", axis=0, tiled=True)

    right = both[:, :, 2:].reshape(2, 2, CORE, CORE, sub, unit).transpose(2, 1, 0, 3, 4, 5)
    right = right.reshape(CORE, 2, 4 * sub, unit)

    def panel(shard):
        whole = jnp.zeros((2, 2, Z_LO, 4 * sub, unit), jnp.bfloat16)
        for d, part in ring(shard):
            origin = (z - d) % Z
            hi, lo = origin // Z_LO, origin % Z_LO
            for k_hi in range(2):
                whole = lax.dynamic_update_slice(
                    whole, part[k_hi][None, None, None], (hi, (k_hi + zhi) % 2, lo, 0, 0)
                )
        whole = whole.reshape(2, 2, Z_LO * 4 * sub, unit)
        return jnp.concatenate([whole[0], whole[1]], -1)

    def product(panel_of):
        return lax.dot_general(
            left_near, panel_of[0], (((0,), (0,)), ((), ())), preferred_element_type=jnp.float32
        ) + lax.dot_general(
            left_far, panel_of[1], (((0,), (0,)), ((), ())), preferred_element_type=jnp.float32
        )

    theirs = panel(pick(right, 1 - core))
    ours = panel(pick(right, core))
    sent = swap(product(theirs).astype(jnp.bfloat16), "core")
    total = product(ours) + sent.astype(jnp.float32)
    total = total.reshape(X, half, 2 * unit)
    rounded = total.astype(jnp.bfloat16)
    partial = pick(total, x)
    for step in range(1, X):
        partial = partial + shift_x(pick(rounded, (x + step) % X), step).astype(jnp.float32)

    squares = jnp.sum(partial * partial, axis=0)
    partial = partial.reshape(half, 2, unit).transpose(1, 0, 2)
    other = swap(pick(partial, 1 - zhi).astype(jnp.bfloat16), "zhi").astype(jnp.float32)
    mine = pick(partial, zhi)
    peers = Z_LO * X * Z_HI
    sums = jnp.broadcast_to(squares, (peers, 1, 2 * unit))
    sums = lax.all_to_all(sums, ("zlo", "x", "zhi"), split_axis=0, concat_axis=0, tiled=True)
    col_total = pick(sums.sum(axis=(0, 1)).reshape(2, unit), zhi)
    col_scale = col_total / (rows * Z_LO * X) + 1e-06
    expanded = jnp.concatenate(
        [jnp.where(zhi == 0, mine, other), jnp.where(zhi == 0, other, mine)], 0
    )
    return spread_tiles(keep_mask, tile_size) * (expanded * expanded) / col_scale[None, :]


def solution(mesh):
    physical = Mesh(
        mesh.devices.reshape(Z_LO, X, Y, Z_HI, CORE), ("zlo", "x", "y", "zhi", "core")
    )
    spec = P(("zlo", "x"), ("y", "zhi", "core"))
    return jax.shard_map(
        local, mesh=physical, in_specs=(spec, spec, spec), out_specs=spec, check_vma=False
    )
```

```python
import jax
import jax.numpy as jnp
from jax import lax
from jax.sharding import Mesh
from jax.sharding import PartitionSpec as P

Z_LO, X, Y, Z_HI, CORE = 4, 4, 8, 2, 2


def spread_tiles(mask, tile_size):
    count_rows, count_cols = mask.shape
    wide = jnp.broadcast_to(
        mask.astype(jnp.float32)[:, None, :, None], (count_rows, tile_size, count_cols, tile_size)
    )
    return wide.reshape(count_rows * tile_size, count_cols * tile_size)


def shift_y(shard, step):
    return lax.ppermute(shard, "y", [(i, (i + step) % Y) for i in range(Y)])


def shift_x(shard, step):
    return lax.ppermute(shard, "x", [(i, (i + step) % X) for i in range(X)])


def swap(shard, axis):
    return lax.ppermute(shard, axis, [(0, 1), (1, 0)])


def pick(stack, index):
    return lax.dynamic_index_in_dim(stack, index, 0, keepdims=False)


def in_order(first, second):
    return lax.optimization_barrier((first, second))


def rings(near, far, shift, size):
    arrived = ([(0, near)], [])
    ends = [[near, near], [far, far]]
    for d in range(1, size // 2):
        for which in (0, 1):
            up, down = ends[which]
            up, down = shift(up, 1), shift(down, -1)
            if d == 1 and which == 0:
                up, far = in_order(up, far)
                ends[1] = [far, far]
                arrived[1].append((0, far))
            ends[which] = [up, down]
            arrived[which].extend([(d, up), (-d, down)])
    half = near.shape[0] // 2
    for which in (0, 1):
        up, down = ends[which]
        last = jnp.concatenate([shift(up[:half], 1), shift(down[half:], -1)], 0)
        arrived[which].append((size // 2, last))
    return arrived


def local(values, tile_mask, keep_mask):
    rows, unit = values.shape
    tile_size = unit // tile_mask.shape[1]
    sub = unit // (X * CORE)
    half = rows // 2
    x, y, core, zhi = (lax.axis_index(a) for a in ("x", "y", "core", "zhi"))
    weighted = (values * spread_tiles(tile_mask, tile_size)).astype(jnp.bfloat16)

    left = weighted.T.reshape(X * CORE, sub, 2, half).transpose(0, 2, 1, 3)
    right = weighted.reshape(CORE, X * CORE, sub, unit).transpose(1, 0, 2, 3)
    both = jnp.concatenate([left, right], 1)
    both = lax.all_to_all(both, ("x", "core"), split_axis=0, concat_axis=0, tiled=True)
    both = both.reshape(X, CORE, 4, sub, unit)

    right = both[:, :, 2:].reshape(2, 2, CORE, CORE, sub, unit).transpose(1, 0, 3, 4, 2, 5)
    right = jnp.where(core == 0, right, right[..., ::-1, :]).reshape(1, 8 * sub, CORE * unit)
    right = lax.all_gather(right, ("zhi", "zlo"), axis=0, tiled=True)
    right = right.reshape(Z_HI, Z_LO * 8 * sub, CORE * unit)

    left = both[:, :, :2].transpose(2, 1, 3, 0, 4).reshape(2, CORE * sub, X * half)
    far = swap(pick(left, 1 - zhi), "zhi")
    whole = jnp.zeros((Y // 2, Z_HI, 2, CORE * sub, X * half), jnp.bfloat16)
    for arrived, hi in zip(rings(pick(left, zhi), far, shift_y, Y), (zhi, 1 - zhi)):
        for d, shard in arrived:
            origin = (y - d) % Y
            whole = lax.dynamic_update_slice(
                whole, shard[None, None, None], (origin // 2, hi, origin % 2, 0, 0)
            )
    left = whole.reshape(Y * Z_HI * CORE * sub, X * half)

    def columns(which):
        product = lax.dot_general(
            left, pick(right, which), (((0,), (0,)), ((), ())), preferred_element_type=jnp.float32
        )
        sent = swap(product[:, unit:].astype(jnp.bfloat16), "core")
        total = product[:, :unit] + sent.astype(jnp.float32)
        total = total.reshape(X, half, unit)
        rounded = total.astype(jnp.bfloat16)
        partial = pick(total, x)
        for step in range(1, X):
            partial = partial + shift_x(pick(rounded, (x + step) % X), step).astype(jnp.float32)
        return partial

    other = columns(1 - zhi)
    sums = swap(jnp.sum(other * other, axis=0)[None], "zhi")
    other = swap(other.astype(jnp.bfloat16), "zhi").astype(jnp.float32)
    mine = columns(zhi)
    sums = sums + jnp.sum(mine * mine, axis=0)[None]
    sums = jnp.broadcast_to(sums, (Z_LO * X, 1, unit))
    sums = lax.all_to_all(sums, ("zlo", "x"), split_axis=0, concat_axis=0, tiled=True)
    col_scale = sums.sum(axis=(0, 1)) / (rows * Z_LO * X) + 1e-06
    expanded = jnp.concatenate(
        [jnp.where(zhi == 0, mine, other), jnp.where(zhi == 0, other, mine)], 0
    )
    return spread_tiles(keep_mask, tile_size) * (expanded * expanded) / col_scale[None, :]


def solution(mesh):
    physical = Mesh(
        mesh.devices.reshape(Z_LO, X, Y, Z_HI, CORE), ("zlo", "x", "y", "zhi", "core")
    )
    spec = P(("zlo", "x"), ("y", "zhi", "core"))
    return jax.shard_map(
        local, mesh=physical, in_specs=(spec, spec, spec), out_specs=spec, check_vma=False
    )
```

```python
import functools

import jax
import jax.numpy as jnp
from jax import lax
from jax.experimental import pallas as pl
from jax.experimental.pallas import tpu as pltpu
from jax.sharding import Mesh
from jax.sharding import PartitionSpec as P

Z_LO, X, Y, Z_HI, CORE = 4, 4, 8, 2, 2
ROWS, UNIT, TILE = 768, 384, 128
HALF = ROWS // 2
SUB = UNIT // (X * CORE)
WIDE = X * HALF
DEPTH = Y * Z_HI * CORE * SUB
VMEM = pl.BlockSpec(memory_space=pltpu.VMEM)
SMEM = pl.BlockSpec(memory_space=pltpu.SMEM)
HBM = pl.BlockSpec(memory_space=pltpu.HBM)
BF16, F32 = jnp.bfloat16, jnp.float32


def call(body, outs, ins, args, scratch=(), flops=0, vmem=48):
    shapes = [jax.ShapeDtypeStruct(shape, dtype) for shape, dtype in outs]
    moved = sum(a.size * a.dtype.itemsize for a in list(args) + shapes)
    return pl.pallas_call(
        body,
        out_shape=shapes,
        in_specs=ins,
        out_specs=[VMEM] * len(outs),
        scratch_shapes=scratch,
        compiler_params=pltpu.CompilerParams(vmem_limit_bytes=vmem << 20),
        cost_estimate=pl.CostEstimate(flops=flops, bytes_accessed=moved, transcendentals=0),
    )(*args)


def shift_y(shard, step):
    return lax.ppermute(shard, "y", [(i, (i + step) % Y) for i in range(Y)])


def shift_x(shard, step):
    return lax.ppermute(shard, "x", [(i, (i + step) % X) for i in range(X)])


def swap(shard, axis):
    return lax.ppermute(shard, axis, [(0, 1), (1, 0)])


def spread_over(array):
    return lax.all_to_all(array, ("x", "core"), split_axis=0, concat_axis=0, tiled=True)


def weigh(place, mask, values, both, far, weighted):
    zhi = place[0]
    for i in range(ROWS // TILE):
        for j in range(UNIT // TILE):
            at = (slice(i * TILE, (i + 1) * TILE), slice(j * TILE, (j + 1) * TILE))
            weighted[at] = values[at] * mask[i, j].astype(F32)
    for chunk in range(X * CORE):
        for part in range(CORE):
            start = part * UNIT + chunk * SUB
            both[chunk, 1 + part] = weighted[start : start + SUB].astype(BF16)
    near = weighted[pl.ds(pl.multiple_of(zhi * HALF, HALF), HALF)].T.astype(BF16)
    for chunk in range(X * CORE):
        both[chunk, 0] = near[chunk * SUB : (chunk + 1) * SUB]
    far[...] = weighted[pl.ds(pl.multiple_of((1 - zhi) * HALF, HALF), HALF)].T.astype(BF16)


def settle(place, both, near, right, stack):
    core = place[1]
    for x in range(X):
        for part in range(CORE):
            near[part * SUB : (part + 1) * SUB, x * HALF : (x + 1) * HALF] = both[x, part, 0]
    for own in range(2):
        source = core if own else 1 - core
        for x in range(X):
            for part in range(CORE):
                at = (x * CORE + part) * SUB
                stack[at : at + SUB] = both[x, source, 1 + part].astype(F32)
        right[0, own * UNIT : (own + 1) * UNIT] = stack[...].T.astype(BF16)


def multiply(order, place, *refs):
    shards, right = refs[: len(order)], refs[len(order)]
    outs, (a, b, sems) = refs[len(order) + 1 : -3], refs[-3:]
    y, zhi = place[0], place[1]
    copies = []
    for shard, (far, d, offset, length) in zip(shards, order):
        k_hi = 1 - zhi if far else zhi
        start = (lax.rem(y + Y - d, Y) * Z_HI + k_hi) * (CORE * SUB) + offset
        start = pl.multiple_of(start, SUB)
        copies.append(
            pltpu.make_async_copy(shard, a.at[pl.ds(start, length)], sems.at[len(copies)])
        )
    for own in range(2):
        for lo in range(Z_LO):
            origin = (zhi if own else 1 - zhi) * Z_LO + lo
            target = b.at[own, :, lo * UNIT : (lo + 1) * UNIT]
            copies.append(pltpu.make_async_copy(right.at[origin], target, sems.at[len(copies)]))
    for copy in copies:
        copy.start()
    for copy in copies[:-Z_LO]:
        copy.wait()
    step = 512
    for own in range(2):
        theirs, ours = outs[2 * own : 2 * own + 2]
        if own:
            for copy in copies[-Z_LO:]:
                copy.wait()

        @pl.loop(0, WIDE // step)
        def _(i):
            at = pl.ds(pl.multiple_of(i * step, step), step)
            product = jnp.dot(b[own], a[:, at], preferred_element_type=F32)
            theirs[:, at] = product[:UNIT].astype(BF16)
            ours[:, at] = product[UNIT:]


def add_core(place, ours, sent, first, second, third, own):
    x = place[0]
    pieces = [own, first, second, third]
    for step in range(X):
        at = pl.ds(pl.multiple_of(lax.rem(x + step, X) * HALF, HALF), HALF)
        total = ours[:, at] + sent[:, at].astype(F32)
        pieces[step][...] = total.astype(pieces[step].dtype)


def add_x(own, first, second, third, total, sums):
    all_x = own[...] + first[...].astype(F32) + (second[...].astype(F32) + third[...].astype(F32))
    turned = all_x.T
    total[...] = turned.astype(total.dtype)
    sums[...] = jnp.sum(turned * turned, axis=0, keepdims=True)


def finish(place, keep, mine, other, sums, flows):
    zhi = place[0]
    scale = jnp.sum(sums[:, 0], axis=0, keepdims=True) / (ROWS * Z_LO * X) + 1e-06
    for own in range(2):
        base = (zhi if own else 1 - zhi) * (HALF // TILE)
        source = mine if own else other
        for i in range(HALF // TILE):
            rows = pl.ds(pl.multiple_of((base + i) * TILE, TILE), TILE)
            for j in range(UNIT // TILE):
                cols = slice(j * TILE, (j + 1) * TILE)
                value = source[i * TILE : (i + 1) * TILE, cols].astype(F32)
                kept = keep[base + i, j].astype(F32)
                flows[rows, cols] = kept * (value * value) / scale[:, cols]


def in_order(first, second):
    return lax.optimization_barrier((first, second))


def rings(near, far):
    shards, order = [near], [(0, 0, 0, CORE * SUB)]
    ends = [[near, near], [far, far]]
    for d in range(1, Y // 2):
        for which in (0, 1):
            up, down = ends[which]
            up, down = shift_y(up, 1), shift_y(down, -1)
            if d == 1 and which == 0:
                up, far = in_order(up, far)
                ends[1] = [far, far]
                shards.append(far)
                order.append((1, 0, 0, CORE * SUB))
            ends[which] = [up, down]
            shards += [up, down]
            order += [(which, d, 0, CORE * SUB), (which, Y - d, 0, CORE * SUB)]
    for which in (0, 1):
        up, down = ends[which]
        shards += [shift_y(up[:SUB], 1), shift_y(down[SUB:], -1)]
        order += [(which, Y // 2, 0, SUB), (which, Y // 2, SUB, SUB)]
    return shards, tuple(order)


def local(values, tile_mask, keep_mask):
    x, y, core, zhi = (lax.axis_index(a) for a in ("x", "y", "core", "zhi"))
    place = jnp.stack([zhi, core])

    both, far = call(
        weigh,
        [((X * CORE, 3, SUB, UNIT), BF16), ((UNIT, HALF), BF16)],
        [SMEM, SMEM, VMEM],
        (place, tile_mask, values),
        [pltpu.VMEM((ROWS, UNIT), F32)],
    )
    far = swap(far, "zhi")
    both = spread_over(both)
    both, far = in_order(both, far)
    far = spread_over(far.reshape(X * CORE, SUB, HALF))
    near, right = call(
        settle,
        [((CORE * SUB, WIDE), BF16), ((1, CORE * UNIT, UNIT), BF16)],
        [SMEM, VMEM],
        (place, both.reshape(X, CORE, 3, SUB, UNIT)),
        [pltpu.VMEM((UNIT, UNIT), F32)],
    )
    right = lax.all_gather(right, ("zhi", "zlo"), axis=0, tiled=True)
    far = far.reshape(X, CORE * SUB, HALF).transpose(1, 0, 2).reshape(CORE * SUB, WIDE)
    shards, order = rings(near, far)

    theirs, ours, theirs_near, ours_near = call(
        functools.partial(multiply, order),
        [((UNIT, WIDE), BF16), ((UNIT, WIDE), F32)] * 2,
        [SMEM] + [HBM] * (len(shards) + 1),
        (jnp.stack([y, zhi]), *shards, right),
        [
            pltpu.VMEM((DEPTH, WIDE), BF16),
            pltpu.VMEM((2, CORE * UNIT, DEPTH), BF16),
            pltpu.SemaphoreType.DMA((len(shards) + 2 * Z_LO,)),
        ],
        flops=4 * CORE * UNIT * DEPTH * WIDE,
        vmem=60,
    )

    def over_x(ours, sent):
        pieces = call(
            add_core,
            [((UNIT, HALF), BF16)] * 3 + [((UNIT, HALF), F32)],
            [SMEM, VMEM, VMEM],
            (x[None], ours, sent),
        )
        return pieces[3], *(shift_x(pieces[step - 1], step) for step in range(1, X))

    def total(pieces, dtype):
        return call(add_x, [((HALF, UNIT), dtype), ((1, UNIT), F32)], [VMEM] * 4, pieces)

    pieces = over_x(ours, swap(theirs, "core"))
    pieces_near = over_x(ours_near, swap(theirs_near, "core"))
    other, sums = total(pieces, BF16)
    sums, other = swap(sums, "zhi"), swap(other, "zhi")
    mine, own_sums = total(pieces_near, F32)
    sums = jnp.broadcast_to(sums + own_sums, (Z_LO * X, 1, UNIT))
    sums = lax.all_to_all(sums, ("zlo", "x"), split_axis=0, concat_axis=0, tiled=True)
    return call(
        finish,
        [((ROWS, UNIT), F32)],
        [SMEM, SMEM, VMEM, VMEM, VMEM],
        (zhi[None], keep_mask, mine, other, sums),
    )[0]


def solution(mesh):
    physical = Mesh(
        mesh.devices.reshape(Z_LO, X, Y, Z_HI, CORE), ("zlo", "x", "y", "zhi", "core")
    )
    spec = P(("zlo", "x"), ("y", "zhi", "core"))
    return jax.shard_map(
        local, mesh=physical, in_specs=(spec, spec, spec), out_specs=spec, check_vma=False
    )
```

```python
import functools

import jax
import jax.numpy as jnp
from jax import lax
from jax.experimental import pallas as pl
from jax.experimental.pallas import tpu as pltpu
from jax.sharding import Mesh
from jax.sharding import PartitionSpec as P

Z_LO, X, Y, Z_HI, CORE = 4, 4, 8, 2, 2
ROWS, UNIT, TILE = 768, 384, 128
HALF = ROWS // 2
SUB = UNIT // (X * CORE)
DEEP = Z_HI * CORE * SUB
DEPTH = Y * DEEP
PARTS = (256, 128)
VMEM = pl.BlockSpec(memory_space=pltpu.VMEM)
SMEM = pl.BlockSpec(memory_space=pltpu.SMEM)
HBM = pl.BlockSpec(memory_space=pltpu.HBM)
BF16, F32 = jnp.bfloat16, jnp.float32


def call(body, outs, ins, args, scratch=(), flops=0, vmem=48):
    shapes = [jax.ShapeDtypeStruct(shape, dtype) for shape, dtype in outs]
    moved = sum(a.size * a.dtype.itemsize for a in list(args) + shapes)
    return pl.pallas_call(
        body,
        out_shape=shapes,
        in_specs=ins,
        out_specs=[VMEM] * len(outs),
        scratch_shapes=scratch,
        compiler_params=pltpu.CompilerParams(vmem_limit_bytes=vmem << 20),
        cost_estimate=pl.CostEstimate(flops=flops, bytes_accessed=moved, transcendentals=0),
    )(*args)


def shift_y(shard, step):
    return lax.ppermute(shard, "y", [(i, (i + step) % Y) for i in range(Y)])


def shift_x(shard, step):
    return lax.ppermute(shard, "x", [(i, (i + step) % X) for i in range(X)])


def swap(shard, axis):
    return lax.ppermute(shard, axis, [(0, 1), (1, 0)])


def spread_over(array):
    return lax.all_to_all(array, ("x", "core"), split_axis=0, concat_axis=0, tiled=True)


def weigh(place, mask, values, right, near, far, weighted):
    zhi = place[0]
    for i in range(ROWS // TILE):
        for j in range(UNIT // TILE):
            at = (slice(i * TILE, (i + 1) * TILE), slice(j * TILE, (j + 1) * TILE))
            weighted[at] = values[at] * mask[i, j].astype(F32)
    for chunk in range(X * CORE):
        for part in range(CORE):
            start = part * UNIT + chunk * SUB
            right[chunk, part] = weighted[start : start + SUB].astype(BF16)
    near[...] = weighted[pl.ds(pl.multiple_of(zhi * HALF, HALF), HALF)].T.astype(BF16)
    far[...] = weighted[pl.ds(pl.multiple_of((1 - zhi) * HALF, HALF), HALF)].T.astype(BF16)


def settle_right(place, both, right, stack):
    core = place[1]
    for own in range(2):
        source = core if own else 1 - core
        for x in range(X):
            for part in range(CORE):
                at = (x * CORE + part) * SUB
                stack[at : at + SUB] = both[x, source, part].astype(F32)
        right[0, own * UNIT : (own + 1) * UNIT] = stack[...].T.astype(BF16)


def settle_left(place, both, *parts):
    zhi = place[0]
    for k_hi in range(Z_HI):
        source = 1 - zhi if k_hi else zhi
        for x in range(X):
            for core in range(CORE):
                rows = slice((k_hi * CORE + core) * SUB, (k_hi * CORE + core + 1) * SUB)
                start = 0
                for part, width in zip(parts, PARTS):
                    cols = slice(x * width, (x + 1) * width)
                    part[rows, cols] = both[x, core, source, :, start : start + width]
                    start += width


def multiply(order, place, *refs):
    shards, right = refs[: len(order)], refs[len(order)]
    theirs, ours, a, b, sems = refs[len(order) + 1 :]
    y = place[0]
    copies = []
    for shard, (d, offset, length) in zip(shards, order):
        start = pl.multiple_of(lax.rem(y + Y - d, Y) * DEEP + offset, DEEP // 2)
        copies.append(
            pltpu.make_async_copy(shard, a.at[pl.ds(start, length)], sems.at[len(copies)])
        )
    for hi in range(Z_HI):
        for lo in range(Z_LO):
            target = b.at[hi, :, lo * UNIT : (lo + 1) * UNIT]
            copies.append(
                pltpu.make_async_copy(right.at[hi * Z_LO + lo], target, sems.at[len(copies)])
            )
    for copy in copies:
        copy.start()
    for copy in copies[:-Z_LO]:
        copy.wait()
    step = 512
    for hi in range(Z_HI):
        if hi:
            for copy in copies[-Z_LO:]:
                copy.wait()

        @pl.loop(0, a.shape[1] // step)
        def _(i):
            at = pl.ds(pl.multiple_of(i * step, step), step)
            product = jnp.dot(b[hi], a[:, at], preferred_element_type=F32)
            theirs[hi * UNIT : (hi + 1) * UNIT, at] = product[:UNIT].astype(BF16)
            ours[hi * UNIT : (hi + 1) * UNIT, at] = product[UNIT:]


def add_core(place, ours, sent, first, second, third, own):
    x = place[0]
    width = own.shape[1]
    pieces = [own, first, second, third]
    for step in range(X):
        at = pl.ds(pl.multiple_of(lax.rem(x + step, X) * width, width), width)
        total = ours[:, at] + sent[:, at].astype(F32)
        pieces[step][...] = total.astype(pieces[step].dtype)


def add_x(place, own, first, second, third, mine, other, sums):
    zhi = place[0]
    for same in range(2):
        hi = zhi if same else 1 - zhi
        at = pl.ds(pl.multiple_of(hi * UNIT, UNIT), UNIT)
        all_x = own[at] + first[at].astype(F32) + (second[at].astype(F32) + third[at].astype(F32))
        turned = all_x.T
        if same:
            mine[...] = turned
        else:
            other[...] = turned.astype(BF16)
        sums[:, at] = jnp.sum(turned * turned, axis=0, keepdims=True)


def finish(place, keep, sums, *refs):
    zhi = place[0]
    parts, flows = refs[:-1], refs[-1]
    at = pl.ds(pl.multiple_of(zhi * UNIT, UNIT), UNIT)
    scale = jnp.sum(sums[:, 0, at], axis=0, keepdims=True) / (ROWS * Z_LO * X) + 1e-06
    for own in range(2):
        tile = (zhi if own else 1 - zhi) * (HALF // TILE)
        for part, width in zip(parts[:2] if own else parts[2:], PARTS):
            for i in range(width // TILE):
                rows = pl.ds(pl.multiple_of(tile * TILE, TILE), TILE)
                for j in range(UNIT // TILE):
                    cols = slice(j * TILE, (j + 1) * TILE)
                    value = part[i * TILE : (i + 1) * TILE, cols].astype(F32)
                    kept = keep[tile, j].astype(F32)
                    flows[rows, cols] = kept * (value * value) / scale[:, cols]
                tile += 1


def in_order(first, second):
    return lax.optimization_barrier((first, second))


def rings(first, second):
    shards, ends = [[first], [second]], [[first, first], [second, second]]
    order = [(0, 0, DEEP)]
    half = DEEP // 2
    arrived = {}
    for d in range(1, Y // 2 + 1):
        for which in range(2):
            if which == 0 and d >= 3:
                arrived[d - 2], ends[0] = in_order(arrived[d - 2], ends[0])
            up, down = ends[which]
            if d == Y // 2:
                up, down = up[:half], down[half:]
            ends[which] = [shift_y(up, 1), shift_y(down, -1)]
            if which == 0:
                shards[0] += ends[0]
            else:
                arrived[d] = ends[1]
        order += [(d, 0, DEEP), (Y - d, 0, DEEP)] if d < Y // 2 else [(d, 0, half), (d, half, half)]
    last = Y // 2
    arrived[last - 1], shards[0][-2:] = in_order(arrived[last - 1], shards[0][-2:])
    for d in range(1, last + 1):
        shards[1] += arrived[d]
    return shards, tuple(order)


def local(values, tile_mask, keep_mask):
    x, y, core, zhi = (lax.axis_index(a) for a in ("x", "y", "core", "zhi"))
    place = jnp.stack([zhi, core])

    right, near, far = call(
        weigh,
        [((X * CORE, CORE, SUB, UNIT), BF16), ((UNIT, HALF), BF16), ((UNIT, HALF), BF16)],
        [SMEM, SMEM, VMEM],
        (place, tile_mask, values),
        [pltpu.VMEM((ROWS, UNIT), F32)],
    )
    far = swap(far, "zhi")
    right = spread_over(right)
    right, far = in_order(right, far)
    left = jnp.stack([piece.reshape(X * CORE, SUB, HALF) for piece in (near, far)], 1)
    left = spread_over(left)
    right = call(
        settle_right,
        [((1, CORE * UNIT, UNIT), BF16)],
        [SMEM, VMEM],
        (place, right.reshape(X, CORE, CORE, SUB, UNIT)),
        [pltpu.VMEM((UNIT, UNIT), F32)],
    )[0]
    right = lax.all_gather(right, ("zhi", "zlo"), axis=0, tiled=True)
    starts = call(
        settle_left,
        [((DEEP, X * width), BF16) for width in PARTS],
        [SMEM, VMEM],
        (place, left.reshape(X, CORE, Z_HI, SUB, HALF)),
    )
    shards, order = rings(*starts)

    def part(shards, width, earlier=None):
        theirs, ours = call(
            functools.partial(multiply, order),
            [((Z_HI * UNIT, X * width), BF16), ((Z_HI * UNIT, X * width), F32)],
            [SMEM] + [HBM] * (len(shards) + 1),
            (y[None], *shards, right),
            [
                pltpu.VMEM((DEPTH, X * width), BF16),
                pltpu.VMEM((Z_HI, CORE * UNIT, DEPTH), BF16),
                pltpu.SemaphoreType.DMA((len(shards) + Z_HI * Z_LO,)),
            ],
            flops=4 * CORE * UNIT * DEPTH * X * width,
            vmem=60,
        )
        if earlier is not None:
            earlier, theirs = in_order(earlier, theirs)
        pieces = call(
            add_core,
            [((Z_HI * UNIT, width), BF16)] * 3 + [((Z_HI * UNIT, width), F32)],
            [SMEM, VMEM, VMEM],
            (x[None], ours, swap(theirs, "core")),
        )
        return pieces, earlier

    def over_x(pieces, width):
        mine, other, sums = call(
            add_x,
            [((width, UNIT), F32), ((width, UNIT), BF16), ((1, Z_HI * UNIT), F32)],
            [SMEM] + [VMEM] * 4,
            (zhi[None], pieces[3], *(shift_x(pieces[step - 1], step) for step in range(1, X))),
        )
        return mine, swap(other, "zhi"), sums

    first, _ = part(shards[0], PARTS[0])
    second, first = part(shards[1], PARTS[1], first)
    done = [over_x(first, PARTS[0]), over_x(second, PARTS[1])]
    mine, other, sums = zip(*done)
    sums = jnp.broadcast_to(sum(sums), (Z_LO * X * Z_HI, 1, Z_HI * UNIT))
    sums = lax.all_to_all(sums, ("zlo", "x", "zhi"), split_axis=0, concat_axis=0, tiled=True)
    return call(
        finish,
        [((ROWS, UNIT), F32)],
        [SMEM, SMEM] + [VMEM] * 5,
        (zhi[None], keep_mask, sums, *mine, *other),
    )[0]


def solution(mesh):
    physical = Mesh(
        mesh.devices.reshape(Z_LO, X, Y, Z_HI, CORE), ("zlo", "x", "y", "zhi", "core")
    )
    spec = P(("zlo", "x"), ("y", "zhi", "core"))
    return jax.shard_map(
        local, mesh=physical, in_specs=(spec, spec, spec), out_specs=spec, check_vma=False
    )
```

```python
import functools

import jax
import jax.numpy as jnp
from jax import lax
from jax.experimental import pallas as pl
from jax.experimental.pallas import tpu as pltpu
from jax.sharding import Mesh
from jax.sharding import PartitionSpec as P

Z_LO, X, Y, Z_HI, CORE = 4, 4, 8, 2, 2
ROWS, UNIT, TILE = 768, 384, 128
HALF = ROWS // 2
SUB = UNIT // (X * CORE)
WIDE = X * HALF
DEPTH = Y * Z_HI * CORE * SUB
VMEM = pl.BlockSpec(memory_space=pltpu.VMEM)
SMEM = pl.BlockSpec(memory_space=pltpu.SMEM)
HBM = pl.BlockSpec(memory_space=pltpu.HBM)
BF16, F32 = jnp.bfloat16, jnp.float32


def call(body, outs, ins, args, scratch=(), flops=0, vmem=48):
    shapes = [jax.ShapeDtypeStruct(shape, dtype) for shape, dtype in outs]
    moved = sum(a.size * a.dtype.itemsize for a in list(args) + shapes)
    return pl.pallas_call(
        body,
        out_shape=shapes,
        in_specs=ins,
        out_specs=[VMEM] * len(outs),
        scratch_shapes=scratch,
        compiler_params=pltpu.CompilerParams(vmem_limit_bytes=vmem << 20),
        cost_estimate=pl.CostEstimate(flops=flops, bytes_accessed=moved, transcendentals=0),
    )(*args)


def shift_y(shard, step):
    return lax.ppermute(shard, "y", [(i, (i + step) % Y) for i in range(Y)])


def shift_x(shard, step):
    return lax.ppermute(shard, "x", [(i, (i + step) % X) for i in range(X)])


def swap(shard, axis):
    return lax.ppermute(shard, axis, [(0, 1), (1, 0)])


def spread_over(array):
    return lax.all_to_all(array, ("x", "core"), split_axis=0, concat_axis=0, tiled=True)


def weigh(place, mask, values, both, far, weighted):
    zhi = place[0]
    for i in range(ROWS // TILE):
        for j in range(UNIT // TILE):
            at = (slice(i * TILE, (i + 1) * TILE), slice(j * TILE, (j + 1) * TILE))
            weighted[at] = values[at] * mask[i, j].astype(F32)
    for chunk in range(X * CORE):
        for part in range(CORE):
            start = part * UNIT + chunk * SUB
            both[chunk, 1 + part] = weighted[start : start + SUB].astype(BF16)
    near = weighted[pl.ds(pl.multiple_of(zhi * HALF, HALF), HALF)].T.astype(BF16)
    for chunk in range(X * CORE):
        both[chunk, 0] = near[chunk * SUB : (chunk + 1) * SUB]
    far[...] = weighted[pl.ds(pl.multiple_of((1 - zhi) * HALF, HALF), HALF)].T.astype(BF16)


def settle(place, both, near, right, stack):
    core = place[1]
    for x in range(X):
        for part in range(CORE):
            near[part * SUB : (part + 1) * SUB, x * HALF : (x + 1) * HALF] = both[x, part, 0]
    for own in range(2):
        source = core if own else 1 - core
        for x in range(X):
            for part in range(CORE):
                at = (x * CORE + part) * SUB
                stack[at : at + SUB] = both[x, source, 1 + part].astype(F32)
        right[0, own * UNIT : (own + 1) * UNIT] = stack[...].T.astype(BF16)


def multiply(order, place, *refs):
    shards, right = refs[: len(order)], refs[len(order)]
    outs, (a, b, sems) = refs[len(order) + 1 : -3], refs[-3:]
    y, zhi = place[0], place[1]
    copies = []
    for shard, (far, d, offset, length) in zip(shards, order):
        k_hi = 1 - zhi if far else zhi
        start = (lax.rem(y + Y - d, Y) * Z_HI + k_hi) * (CORE * SUB) + offset
        start = pl.multiple_of(start, SUB)
        copies.append(
            pltpu.make_async_copy(shard, a.at[pl.ds(start, length)], sems.at[len(copies)])
        )
    for own in range(2):
        for lo in range(Z_LO):
            origin = (zhi if own else 1 - zhi) * Z_LO + lo
            target = b.at[own, :, lo * UNIT : (lo + 1) * UNIT]
            copies.append(pltpu.make_async_copy(right.at[origin], target, sems.at[len(copies)]))
    for copy in copies:
        copy.start()
    for copy in copies[:-Z_LO]:
        copy.wait()
    step = 512
    for own in range(2):
        theirs, ours = outs[2 * own : 2 * own + 2]
        if own:
            for copy in copies[-Z_LO:]:
                copy.wait()

        @pl.loop(0, WIDE // step)
        def _(i):
            at = pl.ds(pl.multiple_of(i * step, step), step)
            product = jnp.dot(b[own], a[:, at], preferred_element_type=F32)
            theirs[:, at] = product[:UNIT].astype(BF16)
            ours[:, at] = product[UNIT:].astype(BF16)


def add_core(ours, sent, pieces):
    for x in range(X):
        at = slice(x * HALF, (x + 1) * HALF)
        pieces[x] = (ours[:, at].astype(F32) + sent[:, at].astype(F32)).astype(BF16)


def add_core_apart(place, ours, sent, *pieces):
    for step in range(X):
        at = pl.ds(pl.multiple_of(lax.rem(place[0] + step, X) * HALF, HALF), HALF)
        pieces[step][...] = (ours[:, at].astype(F32) + sent[:, at].astype(F32)).astype(BF16)


def add_x(*refs):
    pieces, total, sums = refs[:-2], refs[-2], refs[-1]
    if len(pieces) == 1:
        pieces = [pieces[0].at[x] for x in range(X)]
    turned = sum(piece[...].astype(F32) for piece in pieces).T
    total[...] = turned.astype(total.dtype)
    sums[...] = jnp.sum(turned * turned, axis=0, keepdims=True)


def finish(place, keep, mine, other, sums, flows):
    zhi = place[0]
    at = pl.ds(pl.multiple_of(zhi * UNIT, UNIT), UNIT)
    scale = jnp.sum(sums[:, 0, at], axis=0, keepdims=True) / (ROWS * Z_LO * X) + 1e-06
    for own in range(2):
        base = (zhi if own else 1 - zhi) * (HALF // TILE)
        source = mine if own else other
        for i in range(HALF // TILE):
            rows = pl.ds(pl.multiple_of((base + i) * TILE, TILE), TILE)
            for j in range(UNIT // TILE):
                cols = slice(j * TILE, (j + 1) * TILE)
                value = source[i * TILE : (i + 1) * TILE, cols].astype(F32)
                kept = keep[base + i, j].astype(F32)
                flows[rows, cols] = kept * (value * value) / scale[:, cols]


def in_order(first, second):
    return lax.optimization_barrier((first, second))


def rings(near, far):
    shards, order = [near], [(0, 0, 0, CORE * SUB)]
    ends = [[near, near], [far, far]]
    for d in range(1, Y // 2):
        for which in (0, 1):
            up, down = ends[which]
            up, down = shift_y(up, 1), shift_y(down, -1)
            if d == 1 and which == 0:
                up, far = in_order(up, far)
                ends[1] = [far, far]
                shards.append(far)
                order.append((1, 0, 0, CORE * SUB))
            ends[which] = [up, down]
            shards += [up, down]
            order += [(which, d, 0, CORE * SUB), (which, Y - d, 0, CORE * SUB)]
    for which in (0, 1):
        up, down = ends[which]
        shards += [shift_y(up[:SUB], 1), shift_y(down[SUB:], -1)]
        order += [(which, Y // 2, 0, SUB), (which, Y // 2, SUB, SUB)]
    return shards, tuple(order)


def local(values, tile_mask, keep_mask):
    x, y, core, zhi = (lax.axis_index(a) for a in ("x", "y", "core", "zhi"))
    place = jnp.stack([zhi, core])

    both, far = call(
        weigh,
        [((X * CORE, 3, SUB, UNIT), BF16), ((UNIT, HALF), BF16)],
        [SMEM, SMEM, VMEM],
        (place, tile_mask, values),
        [pltpu.VMEM((ROWS, UNIT), F32)],
    )
    far = swap(far, "zhi")
    both = spread_over(both)
    both, far = in_order(both, far)
    far = spread_over(far.reshape(X * CORE, SUB, HALF))
    near, right = call(
        settle,
        [((CORE * SUB, WIDE), BF16), ((1, CORE * UNIT, UNIT), BF16)],
        [SMEM, VMEM],
        (place, both.reshape(X, CORE, 3, SUB, UNIT)),
        [pltpu.VMEM((UNIT, UNIT), F32)],
    )
    right = lax.all_gather(right, ("zhi", "zlo"), axis=0, tiled=True)
    far = far.reshape(X, CORE * SUB, HALF).transpose(1, 0, 2).reshape(CORE * SUB, WIDE)
    shards, order = rings(near, far)

    theirs, ours, theirs_near, ours_near = call(
        functools.partial(multiply, order),
        [((UNIT, WIDE), BF16)] * 4,
        [SMEM] + [HBM] * (len(shards) + 1),
        (jnp.stack([y, zhi]), *shards, right),
        [
            pltpu.VMEM((DEPTH, WIDE), BF16),
            pltpu.VMEM((2, CORE * UNIT, DEPTH), BF16),
            pltpu.SemaphoreType.DMA((len(shards) + 2 * Z_LO,)),
        ],
        flops=4 * CORE * UNIT * DEPTH * WIDE,
        vmem=60,
    )

    def total(pieces, dtype):
        return call(
            add_x, [((HALF, UNIT), dtype), ((1, UNIT), F32)], [VMEM] * len(pieces), pieces
        )

    pieces = call(
        add_core, [((X, UNIT, HALF), BF16)], [VMEM, VMEM], (ours, swap(theirs, "core"))
    )[0]
    pieces = lax.all_to_all(pieces, "x", split_axis=0, concat_axis=0, tiled=True)
    apart = call(
        add_core_apart,
        [((UNIT, HALF), BF16)] * X,
        [SMEM, VMEM, VMEM],
        (x[None], ours_near, swap(theirs_near, "core")),
    )
    apart = [apart[0]] + [shift_x(apart[step], step) for step in range(1, X)]
    (other, sums), apart = in_order(total([pieces], BF16), apart)
    other = swap(other, "zhi")
    mine, own_sums = total(apart, F32)
    sums = jnp.concatenate(
        [jnp.where(zhi == 0, own_sums, sums), jnp.where(zhi == 0, sums, own_sums)], 1
    )
    sums = jnp.broadcast_to(sums, (Z_LO * X * Z_HI, 1, Z_HI * UNIT))
    sums = lax.all_to_all(sums, ("zlo", "x", "zhi"), split_axis=0, concat_axis=0, tiled=True)
    return call(
        finish,
        [((ROWS, UNIT), F32)],
        [SMEM, SMEM, VMEM, VMEM, VMEM],
        (zhi[None], keep_mask, mine, other, sums),
    )[0]


def solution(mesh):
    physical = Mesh(
        mesh.devices.reshape(Z_LO, X, Y, Z_HI, CORE), ("zlo", "x", "y", "zhi", "core")
    )
    spec = P(("zlo", "x"), ("y", "zhi", "core"))
    return jax.shard_map(
        local, mesh=physical, in_specs=(spec, spec, spec), out_specs=spec, check_vma=False
    )
```

```python
import functools

import jax
import jax.numpy as jnp
from jax import lax
from jax.experimental import pallas as pl
from jax.experimental.pallas import tpu as pltpu
from jax.sharding import Mesh
from jax.sharding import PartitionSpec as P

Z_LO, X, Y, Z_HI, CORE = 4, 4, 8, 2, 2
ROWS, UNIT, TILE = 768, 384, 128
HALF = ROWS // 2
SUB = UNIT // (X * CORE)
WIDE = X * HALF
DEPTH = Y * Z_HI * CORE * SUB
VMEM = pl.BlockSpec(memory_space=pltpu.VMEM)
SMEM = pl.BlockSpec(memory_space=pltpu.SMEM)
HBM = pl.BlockSpec(memory_space=pltpu.HBM)
BF16, F32 = jnp.bfloat16, jnp.float32


def call(body, outs, ins, args, scratch=(), flops=0, vmem=48):
    shapes = [jax.ShapeDtypeStruct(shape, dtype) for shape, dtype in outs]
    moved = sum(a.size * a.dtype.itemsize for a in list(args) + shapes)
    return pl.pallas_call(
        body,
        out_shape=shapes,
        in_specs=ins,
        out_specs=[VMEM] * len(outs),
        scratch_shapes=scratch,
        compiler_params=pltpu.CompilerParams(vmem_limit_bytes=vmem << 20),
        cost_estimate=pl.CostEstimate(flops=flops, bytes_accessed=moved, transcendentals=0),
    )(*args)


def shift_y(shard, step):
    return lax.ppermute(shard, "y", [(i, (i + step) % Y) for i in range(Y)])


def shift_x(shard, step):
    return lax.ppermute(shard, "x", [(i, (i + step) % X) for i in range(X)])


def swap(shard, axis):
    return lax.ppermute(shard, axis, [(0, 1), (1, 0)])


def spread_over(array):
    return lax.all_to_all(array, ("x", "core"), split_axis=0, concat_axis=0, tiled=True)


def weigh(place, mask, values, both, far, weighted):
    zhi = place[0]
    for i in range(ROWS // TILE):
        for j in range(UNIT // TILE):
            at = (slice(i * TILE, (i + 1) * TILE), slice(j * TILE, (j + 1) * TILE))
            weighted[at] = values[at] * mask[i, j].astype(F32)
    for chunk in range(X * CORE):
        for part in range(CORE):
            start = part * UNIT + chunk * SUB
            both[chunk, 1 + part] = weighted[start : start + SUB].astype(BF16)
    near = weighted[pl.ds(pl.multiple_of(zhi * HALF, HALF), HALF)].T.astype(BF16)
    for chunk in range(X * CORE):
        both[chunk, 0] = near[chunk * SUB : (chunk + 1) * SUB]
    far[...] = weighted[pl.ds(pl.multiple_of((1 - zhi) * HALF, HALF), HALF)].T.astype(BF16)


def settle(place, both, near, right, stack):
    core = place[1]
    for x in range(X):
        for part in range(CORE):
            near[part * SUB : (part + 1) * SUB, x * HALF : (x + 1) * HALF] = both[x, part, 0]
    for own in range(2):
        source = core if own else 1 - core
        for x in range(X):
            for part in range(CORE):
                at = (x * CORE + part) * SUB
                stack[at : at + SUB] = both[x, source, 1 + part].astype(F32)
        right[0, own * UNIT : (own + 1) * UNIT] = stack[...].T.astype(BF16)


def multiply(order, place, *refs):
    shards, right = refs[: len(order)], refs[len(order)]
    outs, (a, b, sems) = refs[len(order) + 1 : -3], refs[-3:]
    y, zhi = place[0], place[1]
    copies = []
    for shard, (far, d, offset, length) in zip(shards, order):
        k_hi = 1 - zhi if far else zhi
        start = (lax.rem(y + Y - d, Y) * Z_HI + k_hi) * (CORE * SUB) + offset
        start = pl.multiple_of(start, SUB)
        copies.append(
            pltpu.make_async_copy(shard, a.at[pl.ds(start, length)], sems.at[len(copies)])
        )
    for own in range(2):
        for lo in range(Z_LO):
            origin = (zhi if own else 1 - zhi) * Z_LO + lo
            target = b.at[own, :, lo * UNIT : (lo + 1) * UNIT]
            copies.append(pltpu.make_async_copy(right.at[origin], target, sems.at[len(copies)]))
    for copy in copies:
        copy.start()
    for copy in copies[:-Z_LO]:
        copy.wait()
    step = 512
    for own in range(2):
        theirs, ours = outs[2 * own : 2 * own + 2]
        if own:
            for copy in copies[-Z_LO:]:
                copy.wait()

        @pl.loop(0, WIDE // step)
        def _(i):
            at = pl.ds(pl.multiple_of(i * step, step), step)
            product = jnp.dot(b[own], a[:, at], preferred_element_type=F32)
            theirs[:, at] = product[:UNIT].astype(BF16)
            ours[:, at] = product[UNIT:].astype(BF16)


def add_core(place, ours, sent, *pieces):
    for step in range(X):
        at = pl.ds(pl.multiple_of(lax.rem(place[0] + step, X) * HALF, HALF), HALF)
        pieces[step][...] = (ours[:, at].astype(F32) + sent[:, at].astype(F32)).astype(BF16)


def add_x(*refs):
    pieces, total, sums = refs[:X], refs[X], refs[X + 1]
    turned = sum(piece[...].astype(F32) for piece in pieces).T
    total[...] = turned.astype(total.dtype)
    sums[...] = jnp.sum(turned * turned, axis=0, keepdims=True)


def finish(place, keep, mine, other, sums, flows):
    zhi = place[0]
    scale = jnp.sum(sums[:, 0], axis=0, keepdims=True) / (ROWS * Z_LO * X) + 1e-06
    for own in range(2):
        base = (zhi if own else 1 - zhi) * (HALF // TILE)
        source = mine if own else other
        for i in range(HALF // TILE):
            rows = pl.ds(pl.multiple_of((base + i) * TILE, TILE), TILE)
            for j in range(UNIT // TILE):
                cols = slice(j * TILE, (j + 1) * TILE)
                value = source[i * TILE : (i + 1) * TILE, cols].astype(F32)
                kept = keep[base + i, j].astype(F32)
                flows[rows, cols] = kept * (value * value) / scale[:, cols]


def in_order(first, second):
    return lax.optimization_barrier((first, second))


def rings(near, far):
    shards, order = [near], [(0, 0, 0, CORE * SUB)]
    ups, downs = [near, far], [near, far]
    ups[0] = shift_y(near, 1)
    downs[0] = shift_y(near, -1)
    ups[0], far = in_order(ups[0], far)
    shards += [ups[0], downs[0], far]
    order += [(0, 1, 0, CORE * SUB), (0, Y - 1, 0, CORE * SUB), (1, 0, 0, CORE * SUB)]
    ups[1], downs[1] = far, far
    last = Y // 2
    for d in range(2, last + 2):
        cut = [(0, d), (1, d - 1)]
        up, down = list(ups), list(downs)
        for which, distance in cut:
            if distance == last:
                up[which], down[which] = ups[which][:SUB], downs[which][SUB:]
        live = [which for which, distance in cut if distance <= last]
        for which in live:
            ups[which] = shift_y(up[which], 1)
        for which in live:
            downs[which] = shift_y(down[which], -1)
        for which, distance in cut:
            if distance < last:
                order += [(which, distance, 0, CORE * SUB), (which, Y - distance, 0, CORE * SUB)]
            elif distance == last:
                order += [(which, last, 0, SUB), (which, last, SUB, SUB)]
            else:
                continue
            shards += [ups[which], downs[which]]
        if d < last:
            ups[:] = in_order(*ups)
            downs[:] = in_order(*downs)
            shards[-4:] = [ups[0], downs[0], ups[1], downs[1]]
    return shards, tuple(order)


def local(values, tile_mask, keep_mask):
    x, y, core, zhi = (lax.axis_index(a) for a in ("x", "y", "core", "zhi"))
    place = jnp.stack([zhi, core])

    both, far = call(
        weigh,
        [((X * CORE, 3, SUB, UNIT), BF16), ((UNIT, HALF), BF16)],
        [SMEM, SMEM, VMEM],
        (place, tile_mask, values),
        [pltpu.VMEM((ROWS, UNIT), F32)],
    )
    far = swap(far, "zhi")
    both = spread_over(both)
    both, far = in_order(both, far)
    far = spread_over(far.reshape(X * CORE, SUB, HALF))
    near, right = call(
        settle,
        [((CORE * SUB, WIDE), BF16), ((1, CORE * UNIT, UNIT), BF16)],
        [SMEM, VMEM],
        (place, both.reshape(X, CORE, 3, SUB, UNIT)),
        [pltpu.VMEM((UNIT, UNIT), F32)],
    )
    right = lax.all_gather(right, ("zhi", "zlo"), axis=0, tiled=True)
    far = far.reshape(X, CORE * SUB, HALF).transpose(1, 0, 2).reshape(CORE * SUB, WIDE)
    shards, order = rings(near, far)

    theirs, ours, theirs_near, ours_near = call(
        functools.partial(multiply, order),
        [((UNIT, WIDE), BF16)] * 4,
        [SMEM] + [HBM] * (len(shards) + 1),
        (jnp.stack([y, zhi]), *shards, right),
        [
            pltpu.VMEM((DEPTH, WIDE), BF16),
            pltpu.VMEM((2, CORE * UNIT, DEPTH), BF16),
            pltpu.SemaphoreType.DMA((len(shards) + 2 * Z_LO,)),
        ],
        flops=4 * CORE * UNIT * DEPTH * WIDE,
        vmem=60,
    )

    def total(apart, dtype):
        return call(add_x, [((HALF, UNIT), dtype), ((1, UNIT), F32)], [VMEM] * X, apart)

    def over_x(ours, theirs):
        apart = call(
            add_core,
            [((UNIT, HALF), BF16)] * X,
            [SMEM, VMEM, VMEM],
            (x[None], ours, swap(theirs, "core")),
        )
        return [apart[0]] + [shift_x(apart[step], step) for step in range(1, X)]

    apart = over_x(ours, theirs)
    apart_near = over_x(ours_near, theirs_near)
    other, sums = total(apart, BF16)
    sums, other = in_order(swap(sums, "zhi"), other)
    other = swap(other, "zhi")
    mine, own_sums = total(apart_near, F32)
    sums = jnp.broadcast_to(sums + own_sums, (Z_LO * X, 1, UNIT))
    sums = lax.all_to_all(sums, ("zlo", "x"), split_axis=0, concat_axis=0, tiled=True)
    return call(
        finish,
        [((ROWS, UNIT), F32)],
        [SMEM, SMEM, VMEM, VMEM, VMEM],
        (zhi[None], keep_mask, mine, other, sums),
    )[0]


def solution(mesh):
    physical = Mesh(
        mesh.devices.reshape(Z_LO, X, Y, Z_HI, CORE), ("zlo", "x", "y", "zhi", "core")
    )
    spec = P(("zlo", "x"), ("y", "zhi", "core"))
    return jax.shard_map(
        local, mesh=physical, in_specs=(spec, spec, spec), out_specs=spec, check_vma=False
    )
```

```python
import functools

import jax
import jax.numpy as jnp
from jax import lax
from jax.experimental import pallas as pl
from jax.experimental.pallas import tpu as pltpu
from jax.sharding import Mesh
from jax.sharding import PartitionSpec as P

Z_LO, X, Y, Z_HI, CORE = 4, 4, 8, 2, 2
ROWS, UNIT, TILE = 768, 384, 128
HALF = ROWS // 2
SUB = UNIT // (X * CORE)
WIDE = X * HALF
DEPTH = Y * Z_HI * CORE * SUB
VMEM = pl.BlockSpec(memory_space=pltpu.VMEM)
SMEM = pl.BlockSpec(memory_space=pltpu.SMEM)
HBM = pl.BlockSpec(memory_space=pltpu.HBM)
BF16, F32 = jnp.bfloat16, jnp.float32


def call(body, outs, ins, args, scratch=(), flops=0, vmem=48):
    shapes = [jax.ShapeDtypeStruct(shape, dtype) for shape, dtype in outs]
    moved = sum(a.size * a.dtype.itemsize for a in list(args) + shapes)
    return pl.pallas_call(
        body,
        out_shape=shapes,
        in_specs=ins,
        out_specs=[VMEM] * len(outs),
        scratch_shapes=scratch,
        compiler_params=pltpu.CompilerParams(vmem_limit_bytes=vmem << 20),
        cost_estimate=pl.CostEstimate(flops=flops, bytes_accessed=moved, transcendentals=0),
    )(*args)


def shift_y(shard, step):
    return lax.ppermute(shard, "y", [(i, (i + step) % Y) for i in range(Y)])


def shift_x(shard, step):
    return lax.ppermute(shard, "x", [(i, (i + step) % X) for i in range(X)])


def swap(shard, axis):
    return lax.ppermute(shard, axis, [(0, 1), (1, 0)])


def weigh(place, mask, values, both, weighted):
    zhi = place[0]
    for i in range(ROWS // TILE):
        for j in range(UNIT // TILE):
            at = (slice(i * TILE, (i + 1) * TILE), slice(j * TILE, (j + 1) * TILE))
            weighted[at] = values[at] * mask[i, j].astype(F32)
    for chunk in range(X * CORE):
        for part in range(CORE):
            start = part * UNIT + chunk * SUB
            both[chunk, 2 + part] = weighted[start : start + SUB].astype(BF16)
    for far in range(2):
        start = (1 - zhi if far else zhi) * HALF
        left = weighted[pl.ds(pl.multiple_of(start, HALF), HALF)].T.astype(BF16)
        for chunk in range(X * CORE):
            both[chunk, far] = left[chunk * SUB : (chunk + 1) * SUB]


def settle(place, both, near, far, right, stack):
    core = place[1]
    for which, left in enumerate((near, far)):
        for x in range(X):
            for part in range(CORE):
                at = (slice(part * SUB, (part + 1) * SUB), slice(x * HALF, (x + 1) * HALF))
                left[at] = both[x, part, which]
    for own in range(2):
        source = core if own else 1 - core
        for x in range(X):
            for part in range(CORE):
                at = (x * CORE + part) * SUB
                stack[at : at + SUB] = both[x, source, 2 + part].astype(F32)
        right[0, own * UNIT : (own + 1) * UNIT] = stack[...].T.astype(BF16)


def multiply(order, place, *refs):
    shards, right = refs[: len(order)], refs[len(order)]
    outs, (a, b, sems) = refs[len(order) + 1 : -3], refs[-3:]
    y, zhi = place[0], place[1]
    copies = []
    for shard, (far, d, offset, length) in zip(shards, order):
        k_hi = 1 - zhi if far else zhi
        start = (lax.rem(y + Y - d, Y) * Z_HI + k_hi) * (CORE * SUB) + offset
        start = pl.multiple_of(start, SUB)
        copies.append(
            pltpu.make_async_copy(shard, a.at[pl.ds(start, length)], sems.at[len(copies)])
        )
    for own in range(2):
        for lo in range(Z_LO):
            origin = (zhi if own else 1 - zhi) * Z_LO + lo
            target = b.at[own, :, lo * UNIT : (lo + 1) * UNIT]
            copies.append(pltpu.make_async_copy(right.at[origin], target, sems.at[len(copies)]))
    for copy in copies:
        copy.start()
    for copy in copies[:-Z_LO]:
        copy.wait()
    step = 512
    for own in range(2):
        theirs, ours = outs[2 * own : 2 * own + 2]
        if own:
            for copy in copies[-Z_LO:]:
                copy.wait()

        @pl.loop(0, WIDE // step)
        def _(i):
            at = pl.ds(pl.multiple_of(i * step, step), step)
            product = jnp.dot(b[own], a[:, at], preferred_element_type=F32)
            theirs[:, at] = product[:UNIT].astype(BF16)
            ours[:, at] = product[UNIT:].astype(BF16)


def add_core(place, ours, sent, *pieces):
    for step in range(X):
        at = pl.ds(pl.multiple_of(lax.rem(place[0] + step, X) * HALF, HALF), HALF)
        pieces[step][...] = (ours[:, at].astype(F32) + sent[:, at].astype(F32)).astype(BF16)


def add_x(*refs):
    pieces, total, sums = refs[:X], refs[X], refs[X + 1]
    turned = sum(piece[...].astype(F32) for piece in pieces).T
    total[...] = turned.astype(total.dtype)
    sums[...] = jnp.sum(turned * turned, axis=0, keepdims=True)


def finish(place, keep, mine, other, sums, flows):
    zhi = place[0]
    scale = jnp.sum(sums[:, 0], axis=0, keepdims=True) / (ROWS * Z_LO * X) + 1e-06
    for own in range(2):
        base = (zhi if own else 1 - zhi) * (HALF // TILE)
        source = mine if own else other
        for i in range(HALF // TILE):
            rows = pl.ds(pl.multiple_of((base + i) * TILE, TILE), TILE)
            for j in range(UNIT // TILE):
                cols = slice(j * TILE, (j + 1) * TILE)
                value = source[i * TILE : (i + 1) * TILE, cols].astype(F32)
                kept = keep[base + i, j].astype(F32)
                flows[rows, cols] = kept * (value * value) / scale[:, cols]


def in_order(first, second):
    return lax.optimization_barrier((first, second))


def rings(near, far):
    shards, order = [near], [(0, 0, 0, CORE * SUB)]
    ends = [[near, near], [far, far]]
    for d in range(1, Y // 2):
        for which in (0, 1):
            up, down = ends[which]
            up, down = shift_y(up, 1), shift_y(down, -1)
            if d == 1 and which == 0:
                ends[1] = [far, far]
                shards.append(far)
                order.append((1, 0, 0, CORE * SUB))
            ends[which] = [up, down]
            shards += [up, down]
            order += [(which, d, 0, CORE * SUB), (which, Y - d, 0, CORE * SUB)]
    for which in (0, 1):
        up, down = ends[which]
        shards += [shift_y(up[:SUB], 1), shift_y(down[SUB:], -1)]
        order += [(which, Y // 2, 0, SUB), (which, Y // 2, SUB, SUB)]
    return shards, tuple(order)


def local(values, tile_mask, keep_mask):
    x, y, core, zhi = (lax.axis_index(a) for a in ("x", "y", "core", "zhi"))
    place = jnp.stack([zhi, core])

    both = call(
        weigh,
        [((X * CORE, 4, SUB, UNIT), BF16)],
        [SMEM, SMEM, VMEM],
        (place, tile_mask, values),
        [pltpu.VMEM((ROWS, UNIT), F32)],
    )[0]
    both = lax.all_to_all(both, ("x", "core"), split_axis=0, concat_axis=0, tiled=True)
    near, far, right = call(
        settle,
        [((CORE * SUB, WIDE), BF16)] * 2 + [((1, CORE * UNIT, UNIT), BF16)],
        [SMEM, VMEM],
        (place, both.reshape(X, CORE, 4, SUB, UNIT)),
        [pltpu.VMEM((UNIT, UNIT), F32)],
    )
    right = lax.all_gather(right, ("zhi", "zlo"), axis=0, tiled=True)
    shards, order = rings(near, swap(far, "zhi"))

    theirs, ours, theirs_near, ours_near = call(
        functools.partial(multiply, order),
        [((UNIT, WIDE), BF16)] * 4,
        [SMEM] + [HBM] * (len(shards) + 1),
        (jnp.stack([y, zhi]), *shards, right),
        [
            pltpu.VMEM((DEPTH, WIDE), BF16),
            pltpu.VMEM((2, CORE * UNIT, DEPTH), BF16),
            pltpu.SemaphoreType.DMA((len(shards) + 2 * Z_LO,)),
        ],
        flops=4 * CORE * UNIT * DEPTH * WIDE,
        vmem=60,
    )

    def total(apart, dtype):
        return call(add_x, [((HALF, UNIT), dtype), ((1, UNIT), F32)], [VMEM] * X, apart)

    def over_x(ours, theirs):
        apart = call(
            add_core,
            [((UNIT, HALF), BF16)] * X,
            [SMEM, VMEM, VMEM],
            (x[None], ours, swap(theirs, "core")),
        )
        return [apart[0]] + [shift_x(apart[step], step) for step in range(1, X)]

    apart = over_x(ours, theirs)
    apart_near = over_x(ours_near, theirs_near)
    other, sums = total(apart, BF16)
    sums, other = in_order(swap(sums, "zhi"), other)
    other = swap(other, "zhi")
    mine, own_sums = total(apart_near, F32)
    sums = jnp.broadcast_to(sums + own_sums, (Z_LO * X, 1, UNIT))
    sums = lax.all_to_all(sums, ("zlo", "x"), split_axis=0, concat_axis=0, tiled=True)
    return call(
        finish,
        [((ROWS, UNIT), F32)],
        [SMEM, SMEM, VMEM, VMEM, VMEM],
        (zhi[None], keep_mask, mine, other, sums),
    )[0]


def solution(mesh):
    physical = Mesh(
        mesh.devices.reshape(Z_LO, X, Y, Z_HI, CORE), ("zlo", "x", "y", "zhi", "core")
    )
    spec = P(("zlo", "x"), ("y", "zhi", "core"))
    return jax.shard_map(
        local, mesh=physical, in_specs=(spec, spec, spec), out_specs=spec, check_vma=False
    )
```

```python
import functools

import jax
import jax.numpy as jnp
from jax import lax
from jax.experimental import pallas as pl
from jax.experimental.pallas import tpu as pltpu
from jax.sharding import Mesh
from jax.sharding import PartitionSpec as P

Z_LO, X, Y, Z_HI, CORE = 4, 4, 8, 2, 2
ROWS, UNIT, TILE = 768, 384, 128
HALF = ROWS // 2
SUB = UNIT // (X * CORE)
WIDE = X * HALF
DEPTH = Y * Z_HI * CORE * SUB
VMEM = pl.BlockSpec(memory_space=pltpu.VMEM)
SMEM = pl.BlockSpec(memory_space=pltpu.SMEM)
HBM = pl.BlockSpec(memory_space=pltpu.HBM)
BF16, F32 = jnp.bfloat16, jnp.float32


def call(body, outs, ins, args, scratch=(), flops=0, vmem=48):
    shapes = [jax.ShapeDtypeStruct(shape, dtype) for shape, dtype in outs]
    moved = sum(a.size * a.dtype.itemsize for a in list(args) + shapes)
    return pl.pallas_call(
        body,
        out_shape=shapes,
        in_specs=ins,
        out_specs=[VMEM] * len(outs),
        scratch_shapes=scratch,
        compiler_params=pltpu.CompilerParams(vmem_limit_bytes=vmem << 20),
        cost_estimate=pl.CostEstimate(flops=flops, bytes_accessed=moved, transcendentals=0),
    )(*args)


def shift_y(shard, step):
    return lax.ppermute(shard, "y", [(i, (i + step) % Y) for i in range(Y)])


def shift_x(shard, step):
    return lax.ppermute(shard, "x", [(i, (i + step) % X) for i in range(X)])


def swap(shard, axis):
    return lax.ppermute(shard, axis, [(0, 1), (1, 0)])


def spread_over(array):
    return lax.all_to_all(array, ("x", "core"), split_axis=0, concat_axis=0, tiled=True)


def weigh(place, mask, values, both, far, weighted):
    zhi = place[0]
    for i in range(ROWS // TILE):
        for j in range(UNIT // TILE):
            at = (slice(i * TILE, (i + 1) * TILE), slice(j * TILE, (j + 1) * TILE))
            weighted[at] = values[at] * mask[i, j].astype(F32)
    for chunk in range(X * CORE):
        for part in range(CORE):
            start = part * UNIT + chunk * SUB
            both[chunk, 1 + part] = weighted[start : start + SUB].astype(BF16)
    near = weighted[pl.ds(pl.multiple_of(zhi * HALF, HALF), HALF)].T.astype(BF16)
    for chunk in range(X * CORE):
        both[chunk, 0] = near[chunk * SUB : (chunk + 1) * SUB]
    far[...] = weighted[pl.ds(pl.multiple_of((1 - zhi) * HALF, HALF), HALF)].T.astype(BF16)


def settle(place, both, near, right, stack):
    core = place[1]
    for x in range(X):
        for part in range(CORE):
            near[part * SUB : (part + 1) * SUB, x * HALF : (x + 1) * HALF] = both[x, part, 0]
    for own in range(2):
        source = core if own else 1 - core
        for x in range(X):
            for part in range(CORE):
                at = (x * CORE + part) * SUB
                stack[at : at + SUB] = both[x, source, 1 + part].astype(F32)
        right[0, own * UNIT : (own + 1) * UNIT] = stack[...].T.astype(BF16)


def multiply(order, place, *refs):
    shards, right = refs[: len(order)], refs[len(order)]
    outs, (a, b, sems) = refs[len(order) + 1 : -3], refs[-3:]
    y, zhi = place[0], place[1]
    copies = []
    for shard, (far, d, offset, length) in zip(shards, order):
        k_hi = 1 - zhi if far else zhi
        start = (lax.rem(y + Y - d, Y) * Z_HI + k_hi) * (CORE * SUB) + offset
        start = pl.multiple_of(start, SUB)
        copies.append(
            pltpu.make_async_copy(shard, a.at[pl.ds(start, length)], sems.at[len(copies)])
        )
    for own in range(2):
        for lo in range(Z_LO):
            origin = (zhi if own else 1 - zhi) * Z_LO + lo
            target = b.at[own, :, lo * UNIT : (lo + 1) * UNIT]
            copies.append(pltpu.make_async_copy(right.at[origin], target, sems.at[len(copies)]))
    for copy in copies:
        copy.start()
    for copy in copies[:-Z_LO]:
        copy.wait()
    step = 512
    for own in range(2):
        theirs, ours = outs[2 * own : 2 * own + 2]
        if own:
            for copy in copies[-Z_LO:]:
                copy.wait()

        @pl.loop(0, WIDE // step)
        def _(i):
            at = pl.ds(pl.multiple_of(i * step, step), step)
            product = jnp.dot(b[own], a[:, at], preferred_element_type=F32)
            theirs[:, at] = product[:UNIT].astype(BF16)
            ours[:, at] = product[UNIT:].astype(BF16)


def add_core(place, ours, sent, *pieces):
    for step in range(X):
        at = pl.ds(pl.multiple_of(lax.rem(place[0] + step, X) * HALF, HALF), HALF)
        pieces[step][...] = (ours[:, at].astype(F32) + sent[:, at].astype(F32)).astype(BF16)


def add_x(*refs):
    pieces, total, sums = refs[:X], refs[X], refs[X + 1]
    turned = sum(piece[...].astype(F32) for piece in pieces).T
    total[...] = turned.astype(total.dtype)
    sums[...] = jnp.sum(turned * turned, axis=0, keepdims=True)


def finish(place, keep, mine, other, sums, flows):
    zhi = place[0]
    scale = jnp.sum(sums[:, 0], axis=0, keepdims=True) / (ROWS * Z_LO * X) + 1e-06
    for own in range(2):
        base = (zhi if own else 1 - zhi) * (HALF // TILE)
        source = mine if own else other
        for i in range(HALF // TILE):
            rows = pl.ds(pl.multiple_of((base + i) * TILE, TILE), TILE)
            for j in range(UNIT // TILE):
                cols = slice(j * TILE, (j + 1) * TILE)
                value = source[i * TILE : (i + 1) * TILE, cols].astype(F32)
                kept = keep[base + i, j].astype(F32)
                flows[rows, cols] = kept * (value * value) / scale[:, cols]


def in_order(first, second):
    return lax.optimization_barrier((first, second))


def rings(near, far):
    shards, order = [near], [(0, 0, 0, CORE * SUB)]
    ends = [[near, near], [far, far]]
    for d in range(1, Y // 2):
        for which in (0, 1):
            up, down = ends[which]
            up, down = shift_y(up, 1), shift_y(down, -1)
            if d == 1 and which == 0:
                up, far = in_order(up, far)
                ends[1] = [far, far]
                shards.append(far)
                order.append((1, 0, 0, CORE * SUB))
            ends[which] = [up, down]
            shards += [up, down]
            order += [(which, d, 0, CORE * SUB), (which, Y - d, 0, CORE * SUB)]
    for which in (0, 1):
        up, down = ends[which]
        shards += [shift_y(up[:SUB], 1), shift_y(down[SUB:], -1)]
        order += [(which, Y // 2, 0, SUB), (which, Y // 2, SUB, SUB)]
    return shards, tuple(order)


def local(values, tile_mask, keep_mask):
    x, y, core, zhi = (lax.axis_index(a) for a in ("x", "y", "core", "zhi"))
    place = jnp.stack([zhi, core])

    both, far = call(
        weigh,
        [((X * CORE, 3, SUB, UNIT), BF16), ((UNIT, HALF), BF16)],
        [SMEM, SMEM, VMEM],
        (place, tile_mask, values),
        [pltpu.VMEM((ROWS, UNIT), F32)],
    )
    far = swap(far, "zhi")
    both = spread_over(both)
    both, far = in_order(both, far)
    far = spread_over(far.reshape(X * CORE, SUB, HALF))
    near, right = call(
        settle,
        [((CORE * SUB, WIDE), BF16), ((1, CORE * UNIT, UNIT), BF16)],
        [SMEM, VMEM],
        (place, both.reshape(X, CORE, 3, SUB, UNIT)),
        [pltpu.VMEM((UNIT, UNIT), F32)],
    )
    right = lax.all_gather(right, ("zhi", "zlo"), axis=0, tiled=True)
    far = far.reshape(X, CORE * SUB, HALF).transpose(1, 0, 2).reshape(CORE * SUB, WIDE)
    shards, order = rings(near, far)

    theirs, ours, theirs_near, ours_near = call(
        functools.partial(multiply, order),
        [((UNIT, WIDE), BF16)] * 4,
        [SMEM] + [HBM] * (len(shards) + 1),
        (jnp.stack([y, zhi]), *shards, right),
        [
            pltpu.VMEM((DEPTH, WIDE), BF16),
            pltpu.VMEM((2, CORE * UNIT, DEPTH), BF16),
            pltpu.SemaphoreType.DMA((len(shards) + 2 * Z_LO,)),
        ],
        flops=4 * CORE * UNIT * DEPTH * WIDE,
        vmem=60,
    )

    def total(apart, dtype):
        return call(add_x, [((HALF, UNIT), dtype), ((1, UNIT), F32)], [VMEM] * X, apart)

    def over_x(ours, theirs):
        apart = call(
            add_core,
            [((UNIT, HALF), BF16)] * X,
            [SMEM, VMEM, VMEM],
            (x[None], ours, swap(theirs, "core")),
        )
        return [apart[0]] + [shift_x(apart[step], step) for step in range(1, X)]

    apart = over_x(ours, theirs)
    apart_near = over_x(ours_near, theirs_near)
    other, sums = total(apart, BF16)
    sums, other = in_order(swap(sums, "zhi"), other)
    other = swap(other, "zhi")
    mine, own_sums = total(apart_near, F32)
    sums = jnp.broadcast_to(sums + own_sums, (Z_LO * X, 1, UNIT))
    sums = lax.all_to_all(sums, ("zlo", "x"), split_axis=0, concat_axis=0, tiled=True)
    return call(
        finish,
        [((ROWS, UNIT), F32)],
        [SMEM, SMEM, VMEM, VMEM, VMEM],
        (zhi[None], keep_mask, mine, other, sums),
    )[0]


def solution(mesh):
    physical = Mesh(
        mesh.devices.reshape(Z_LO, X, Y, Z_HI, CORE), ("zlo", "x", "y", "zhi", "core")
    )
    spec = P(("zlo", "x"), ("y", "zhi", "core"))
    return jax.shard_map(
        local, mesh=physical, in_specs=(spec, spec, spec), out_specs=spec, check_vma=False
    )
```

```python
import functools

import jax
import jax.numpy as jnp
from jax import lax
from jax.experimental import pallas as pl
from jax.experimental.pallas import tpu as pltpu
from jax.sharding import Mesh
from jax.sharding import PartitionSpec as P

Z_LO, X, Y, Z_HI, CORE = 4, 4, 8, 2, 2
ROWS, UNIT, TILE = 768, 384, 128
HALF = ROWS // 2
SUB = UNIT // (X * CORE)
WIDE = X * HALF
DEPTH = Y * Z_HI * CORE * SUB
VMEM = pl.BlockSpec(memory_space=pltpu.VMEM)
SMEM = pl.BlockSpec(memory_space=pltpu.SMEM)
HBM = pl.BlockSpec(memory_space=pltpu.HBM)
BF16, F32 = jnp.bfloat16, jnp.float32
SUMS = 16


def call(body, outs, ins, args, scratch=(), flops=0, vmem=48):
    shapes = [jax.ShapeDtypeStruct(shape, dtype) for shape, dtype in outs]
    moved = sum(a.size * a.dtype.itemsize for a in list(args) + shapes)
    return pl.pallas_call(
        body,
        out_shape=shapes,
        in_specs=ins,
        out_specs=[VMEM] * len(outs),
        scratch_shapes=scratch,
        compiler_params=pltpu.CompilerParams(vmem_limit_bytes=vmem << 20),
        cost_estimate=pl.CostEstimate(flops=flops, bytes_accessed=moved, transcendentals=0),
    )(*args)


def shift_y(shard, step):
    return lax.ppermute(shard, "y", [(i, (i + step) % Y) for i in range(Y)])


def shift_x(shard, step):
    return lax.ppermute(shard, "x", [(i, (i + step) % X) for i in range(X)])


def swap(shard, axis):
    return lax.ppermute(shard, axis, [(0, 1), (1, 0)])


def spread_over(array):
    return lax.all_to_all(array, ("x", "core"), split_axis=0, concat_axis=0, tiled=True)


def weigh(place, mask, values, both, far, weighted):
    zhi = place[0]
    for i in range(ROWS // TILE):
        for j in range(UNIT // TILE):
            at = (slice(i * TILE, (i + 1) * TILE), slice(j * TILE, (j + 1) * TILE))
            weighted[at] = values[at] * mask[i, j].astype(F32)
    for chunk in range(X * CORE):
        for part in range(CORE):
            start = part * UNIT + chunk * SUB
            both[chunk, 1 + part] = weighted[start : start + SUB].astype(BF16)
    near = weighted[pl.ds(pl.multiple_of(zhi * HALF, HALF), HALF)].T.astype(BF16)
    for chunk in range(X * CORE):
        both[chunk, 0] = near[chunk * SUB : (chunk + 1) * SUB]
    far[...] = weighted[pl.ds(pl.multiple_of((1 - zhi) * HALF, HALF), HALF)].T.astype(BF16)


def settle(place, both, near, right, stack):
    core = place[1]
    for x in range(X):
        for part in range(CORE):
            near[part * SUB : (part + 1) * SUB, x * HALF : (x + 1) * HALF] = both[x, part, 0]
    for own in range(2):
        source = core if own else 1 - core
        for x in range(X):
            for part in range(CORE):
                at = (x * CORE + part) * SUB
                stack[at : at + SUB] = both[x, source, 1 + part].astype(F32)
        right[0, own * UNIT : (own + 1) * UNIT] = stack[...].T.astype(BF16)


def multiply(order, place, *refs):
    shards, right = refs[: len(order)], refs[len(order)]
    outs, (a, b, sems) = refs[len(order) + 1 : -3], refs[-3:]
    y, zhi = place[0], place[1]
    copies = []
    for shard, (far, d, offset, length) in zip(shards, order):
        k_hi = 1 - zhi if far else zhi
        start = (lax.rem(y + Y - d, Y) * Z_HI + k_hi) * (CORE * SUB) + offset
        start = pl.multiple_of(start, SUB)
        copies.append(
            pltpu.make_async_copy(shard, a.at[pl.ds(start, length)], sems.at[len(copies)])
        )
    for own in range(2):
        for lo in range(Z_LO):
            origin = (zhi if own else 1 - zhi) * Z_LO + lo
            target = b.at[own, :, lo * UNIT : (lo + 1) * UNIT]
            copies.append(pltpu.make_async_copy(right.at[origin], target, sems.at[len(copies)]))
    for copy in copies:
        copy.start()
    for copy in copies[:-Z_LO]:
        copy.wait()
    step = 512
    for own in range(2):
        theirs, ours = outs[2 * own : 2 * own + 2]
        if own:
            for copy in copies[-Z_LO:]:
                copy.wait()

        @pl.loop(0, WIDE // step)
        def _(i):
            at = pl.ds(pl.multiple_of(i * step, step), step)
            product = jnp.dot(b[own], a[:, at], preferred_element_type=F32)
            theirs[:, at] = product[:UNIT].astype(BF16)
            ours[:, at] = product[UNIT:].astype(BF16)


def add_core(place, ours, sent, *pieces):
    for step in range(X):
        at = pl.ds(pl.multiple_of(lax.rem(place[0] + step, X) * HALF, HALF), HALF)
        pieces[step][...] = (ours[:, at].astype(F32) + sent[:, at].astype(F32)).astype(BF16)


def summed(pieces):
    turned = sum(piece[...].astype(F32) for piece in pieces).T
    return turned, jnp.sum(turned * turned, axis=0, keepdims=True)


def add_x(*refs):
    pieces, total, sums = refs[:X], refs[X], refs[X + 1]
    total[...], sums[...] = summed(pieces)


def add_x_to_send(*refs):
    pieces, total = refs[:X], refs[X]
    turned, rest = summed(pieces)
    total[:HALF] = turned.astype(BF16)
    row = lax.broadcasted_iota(jnp.int32, (SUMS, UNIT), 0)
    split = jnp.zeros((SUMS, UNIT), F32)
    for which in range(3):
        part = rest.astype(BF16).astype(F32)
        split = jnp.where(row == which, part, split)
        rest = rest - part
    total[HALF:] = split.astype(BF16)


def finish(place, keep, mine, other, sums, flows):
    zhi = place[0]
    scale = jnp.sum(sums[:, 0], axis=0, keepdims=True) / (ROWS * Z_LO * X) + 1e-06
    for own in range(2):
        base = (zhi if own else 1 - zhi) * (HALF // TILE)
        source = mine if own else other
        for i in range(HALF // TILE):
            rows = pl.ds(pl.multiple_of((base + i) * TILE, TILE), TILE)
            for j in range(UNIT // TILE):
                cols = slice(j * TILE, (j + 1) * TILE)
                value = source[i * TILE : (i + 1) * TILE, cols].astype(F32)
                kept = keep[base + i, j].astype(F32)
                flows[rows, cols] = kept * (value * value) / scale[:, cols]


def in_order(first, second):
    return lax.optimization_barrier((first, second))


def rings(near, far):
    shards, order = [near], [(0, 0, 0, CORE * SUB)]
    ends = [[near, near], [far, far]]
    for d in range(1, Y // 2):
        for which in (0, 1):
            up, down = ends[which]
            up, down = shift_y(up, 1), shift_y(down, -1)
            if d == 1 and which == 0:
                up, far = in_order(up, far)
                ends[1] = [far, far]
                shards.append(far)
                order.append((1, 0, 0, CORE * SUB))
            ends[which] = [up, down]
            shards += [up, down]
            order += [(which, d, 0, CORE * SUB), (which, Y - d, 0, CORE * SUB)]
    shards += [shift_y(ends[0][1], -1), shift_y(ends[1][0], 1)]
    order += [(0, Y // 2, 0, CORE * SUB), (1, Y // 2, 0, CORE * SUB)]
    return shards, tuple(order)


def local(values, tile_mask, keep_mask):
    x, y, core, zhi = (lax.axis_index(a) for a in ("x", "y", "core", "zhi"))
    place = jnp.stack([zhi, core])

    both, far = call(
        weigh,
        [((X * CORE, 3, SUB, UNIT), BF16), ((UNIT, HALF), BF16)],
        [SMEM, SMEM, VMEM],
        (place, tile_mask, values),
        [pltpu.VMEM((ROWS, UNIT), F32)],
    )
    far = swap(far, "zhi")
    both = spread_over(both)
    both, far = in_order(both, far)
    far = spread_over(far.reshape(X * CORE, SUB, HALF))
    near, right = call(
        settle,
        [((CORE * SUB, WIDE), BF16), ((1, CORE * UNIT, UNIT), BF16)],
        [SMEM, VMEM],
        (place, both.reshape(X, CORE, 3, SUB, UNIT)),
        [pltpu.VMEM((UNIT, UNIT), F32)],
    )
    right = lax.all_gather(right, ("zhi", "zlo"), axis=0, tiled=True)
    far = far.reshape(X, CORE * SUB, HALF).transpose(1, 0, 2).reshape(CORE * SUB, WIDE)
    shards, order = rings(near, far)

    theirs, ours, theirs_near, ours_near = call(
        functools.partial(multiply, order),
        [((UNIT, WIDE), BF16)] * 4,
        [SMEM] + [HBM] * (len(shards) + 1),
        (jnp.stack([y, zhi]), *shards, right),
        [
            pltpu.VMEM((DEPTH, WIDE), BF16),
            pltpu.VMEM((2, CORE * UNIT, DEPTH), BF16),
            pltpu.SemaphoreType.DMA((len(shards) + 2 * Z_LO,)),
        ],
        flops=4 * CORE * UNIT * DEPTH * WIDE,
        vmem=60,
    )

    def over_cores(ours, theirs):
        return call(
            add_core,
            [((UNIT, HALF), BF16)] * X,
            [SMEM, VMEM, VMEM],
            (x[None], ours, swap(theirs, "core")),
        )

    def over_x(apart):
        return [apart[0]] + [shift_x(apart[step], step) for step in range(1, X)]

    apart = over_x(over_cores(ours, theirs))
    apart_near, apart = in_order(over_cores(ours_near, theirs_near), apart)
    apart_near = over_x(apart_near)
    other = call(add_x_to_send, [((HALF + SUMS, UNIT), BF16)], [VMEM] * X, apart)[0]
    other = swap(other, "zhi")
    mine, sums = call(add_x, [((HALF, UNIT), F32), ((1, UNIT), F32)], [VMEM] * X, apart_near)
    sums = sums + other[HALF : HALF + 3].astype(F32).sum(axis=0, keepdims=True)
    sums = jnp.broadcast_to(sums, (Z_LO * X, 1, UNIT))
    sums = lax.all_to_all(sums, ("zlo", "x"), split_axis=0, concat_axis=0, tiled=True)
    return call(
        finish,
        [((ROWS, UNIT), F32)],
        [SMEM, SMEM, VMEM, VMEM, VMEM],
        (zhi[None], keep_mask, mine, other, sums),
    )[0]


def solution(mesh):
    physical = Mesh(
        mesh.devices.reshape(Z_LO, X, Y, Z_HI, CORE), ("zlo", "x", "y", "zhi", "core")
    )
    spec = P(("zlo", "x"), ("y", "zhi", "core"))
    return jax.shard_map(
        local, mesh=physical, in_specs=(spec, spec, spec), out_specs=spec, check_vma=False
    )
```

```python
import functools

import jax
import jax.numpy as jnp
from jax import lax
from jax.experimental import pallas as pl
from jax.experimental.pallas import tpu as pltpu
from jax.sharding import Mesh
from jax.sharding import PartitionSpec as P

Z_LO, X, Y, Z_HI, CORE = 4, 4, 8, 2, 2
ROWS, UNIT, TILE = 768, 384, 128
HALF = ROWS // 2
SUB = UNIT // (X * CORE)
WIDE = X * HALF
DEPTH = Y * Z_HI * CORE * SUB
VMEM = pl.BlockSpec(memory_space=pltpu.VMEM)
SMEM = pl.BlockSpec(memory_space=pltpu.SMEM)
HBM = pl.BlockSpec(memory_space=pltpu.HBM)
BF16, F32 = jnp.bfloat16, jnp.float32


def call(body, outs, ins, args, scratch=(), flops=0, vmem=48):
    shapes = [jax.ShapeDtypeStruct(shape, dtype) for shape, dtype in outs]
    moved = sum(a.size * a.dtype.itemsize for a in list(args) + shapes)
    return pl.pallas_call(
        body,
        out_shape=shapes,
        in_specs=ins,
        out_specs=[VMEM] * len(outs),
        scratch_shapes=scratch,
        compiler_params=pltpu.CompilerParams(vmem_limit_bytes=vmem << 20),
        cost_estimate=pl.CostEstimate(flops=flops, bytes_accessed=moved, transcendentals=0),
    )(*args)


def shift_y(shard, step):
    return lax.ppermute(shard, "y", [(i, (i + step) % Y) for i in range(Y)])


def shift_x(shard, step):
    return lax.ppermute(shard, "x", [(i, (i + step) % X) for i in range(X)])


def swap(shard, axis):
    return lax.ppermute(shard, axis, [(0, 1), (1, 0)])


def spread_over(array):
    return lax.all_to_all(array, ("x", "core"), split_axis=0, concat_axis=0, tiled=True)


def weigh(place, mask, values, both, far, weighted):
    zhi = place[0]
    for i in range(ROWS // TILE):
        for j in range(UNIT // TILE):
            at = (slice(i * TILE, (i + 1) * TILE), slice(j * TILE, (j + 1) * TILE))
            weighted[at] = values[at] * mask[i, j].astype(F32)
    for chunk in range(X * CORE):
        for part in range(CORE):
            start = part * UNIT + chunk * SUB
            both[chunk, 1 + part] = weighted[start : start + SUB].astype(BF16)
    near = weighted[pl.ds(pl.multiple_of(zhi * HALF, HALF), HALF)].T.astype(BF16)
    for chunk in range(X * CORE):
        both[chunk, 0] = near[chunk * SUB : (chunk + 1) * SUB]
    far[...] = weighted[pl.ds(pl.multiple_of((1 - zhi) * HALF, HALF), HALF)].T.astype(BF16)


def settle(place, both, near, right, stack):
    core = place[1]
    for x in range(X):
        for part in range(CORE):
            near[part * SUB : (part + 1) * SUB, x * HALF : (x + 1) * HALF] = both[x, part, 0]
    for own in range(2):
        source = core if own else 1 - core
        for x in range(X):
            for part in range(CORE):
                at = (x * CORE + part) * SUB
                stack[at : at + SUB] = both[x, source, 1 + part].astype(F32)
        right[0, own * UNIT : (own + 1) * UNIT] = stack[...].T.astype(BF16)


def multiply(order, place, *refs):
    shards, right = refs[: len(order)], refs[len(order)]
    outs, (a, b, sems) = refs[len(order) + 1 : -3], refs[-3:]
    y, zhi = place[0], place[1]
    copies = []
    for shard, (far, d, offset, length) in zip(shards, order):
        k_hi = 1 - zhi if far else zhi
        start = (lax.rem(y + Y - d, Y) * Z_HI + k_hi) * (CORE * SUB) + offset
        start = pl.multiple_of(start, SUB)
        copies.append(
            pltpu.make_async_copy(shard, a.at[pl.ds(start, length)], sems.at[len(copies)])
        )
    for own in range(2):
        for lo in range(Z_LO):
            origin = (zhi if own else 1 - zhi) * Z_LO + lo
            target = b.at[own, :, lo * UNIT : (lo + 1) * UNIT]
            copies.append(pltpu.make_async_copy(right.at[origin], target, sems.at[len(copies)]))
    for copy in copies:
        copy.start()
    for copy in copies[:-Z_LO]:
        copy.wait()
    step = 512
    for own in range(2):
        theirs, ours = outs[2 * own : 2 * own + 2]
        if own:
            for copy in copies[-Z_LO:]:
                copy.wait()

        @pl.loop(0, WIDE // step)
        def _(i):
            at = pl.ds(pl.multiple_of(i * step, step), step)
            product = jnp.dot(b[own], a[:, at], preferred_element_type=F32)
            theirs[:, at] = product[:UNIT].astype(BF16)
            ours[:, at] = product[UNIT:].astype(BF16)


def add_core(place, ours, sent, *pieces):
    for step in range(X):
        at = pl.ds(pl.multiple_of(lax.rem(place[0] + step, X) * HALF, HALF), HALF)
        pieces[step][...] = (ours[:, at].astype(F32) + sent[:, at].astype(F32)).astype(BF16)


def add_x(*refs):
    pieces, total, sums = refs[:X], refs[X], refs[X + 1]
    turned = sum(piece[...].astype(F32) for piece in pieces).T
    total[...] = turned.astype(total.dtype)
    sums[...] = jnp.sum(turned * turned, axis=0, keepdims=True)


def finish(place, keep, mine, other, sums, flows):
    zhi = place[0]
    scale = jnp.sum(sums[:, 0], axis=0, keepdims=True) / (ROWS * Z_LO * X) + 1e-06
    for own in range(2):
        base = (zhi if own else 1 - zhi) * (HALF // TILE)
        source = mine if own else other
        for i in range(HALF // TILE):
            rows = pl.ds(pl.multiple_of((base + i) * TILE, TILE), TILE)
            for j in range(UNIT // TILE):
                cols = slice(j * TILE, (j + 1) * TILE)
                value = source[i * TILE : (i + 1) * TILE, cols].astype(F32)
                kept = keep[base + i, j].astype(F32)
                flows[rows, cols] = kept * (value * value) / scale[:, cols]


def in_order(first, second):
    return lax.optimization_barrier((first, second))


def rings(near, far):
    shards, order = [near], [(0, 0, 0, CORE * SUB)]
    ends = [[near, near], [far, far]]
    for d in range(1, Y // 2):
        for which in (0, 1):
            up, down = ends[which]
            up, down = shift_y(up, 1), shift_y(down, -1)
            if d == 1 and which == 0:
                up, far = in_order(up, far)
                ends[1] = [far, far]
                shards.append(far)
                order.append((1, 0, 0, CORE * SUB))
            ends[which] = [up, down]
            shards += [up, down]
            order += [(which, d, 0, CORE * SUB), (which, Y - d, 0, CORE * SUB)]
    shards += [shift_y(ends[0][1], -1), shift_y(ends[1][0], 1)]
    order += [(0, Y // 2, 0, CORE * SUB), (1, Y // 2, 0, CORE * SUB)]
    return shards, tuple(order)


def local(values, tile_mask, keep_mask):
    x, y, core, zhi = (lax.axis_index(a) for a in ("x", "y", "core", "zhi"))
    place = jnp.stack([zhi, core])

    both, far = call(
        weigh,
        [((X * CORE, 3, SUB, UNIT), BF16), ((UNIT, HALF), BF16)],
        [SMEM, SMEM, VMEM],
        (place, tile_mask, values),
        [pltpu.VMEM((ROWS, UNIT), F32)],
    )
    far = swap(far, "zhi")
    both = spread_over(both)
    both, far = in_order(both, far)
    far = spread_over(far.reshape(X * CORE, SUB, HALF))
    near, right = call(
        settle,
        [((CORE * SUB, WIDE), BF16), ((1, CORE * UNIT, UNIT), BF16)],
        [SMEM, VMEM],
        (place, both.reshape(X, CORE, 3, SUB, UNIT)),
        [pltpu.VMEM((UNIT, UNIT), F32)],
    )
    right = lax.all_gather(right, ("zhi", "zlo"), axis=0, tiled=True)
    far = far.reshape(X, CORE * SUB, HALF).transpose(1, 0, 2).reshape(CORE * SUB, WIDE)
    shards, order = rings(near, far)

    theirs, ours, theirs_near, ours_near = call(
        functools.partial(multiply, order),
        [((UNIT, WIDE), BF16)] * 4,
        [SMEM] + [HBM] * (len(shards) + 1),
        (jnp.stack([y, zhi]), *shards, right),
        [
            pltpu.VMEM((DEPTH, WIDE), BF16),
            pltpu.VMEM((2, CORE * UNIT, DEPTH), BF16),
            pltpu.SemaphoreType.DMA((len(shards) + 2 * Z_LO,)),
        ],
        flops=4 * CORE * UNIT * DEPTH * WIDE,
        vmem=60,
    )

    def total(apart, dtype):
        return call(add_x, [((HALF, UNIT), dtype), ((1, UNIT), F32)], [VMEM] * X, apart)

    def over_x(ours, theirs):
        apart = call(
            add_core,
            [((UNIT, HALF), BF16)] * X,
            [SMEM, VMEM, VMEM],
            (x[None], ours, swap(theirs, "core")),
        )
        return [apart[0]] + [shift_x(apart[step], step) for step in range(1, X)]

    apart = over_x(ours, theirs)
    apart_near = over_x(ours_near, theirs_near)
    other, sums = total(apart, BF16)
    sums, other = in_order(swap(sums, "zhi"), other)
    other = swap(other, "zhi")
    mine, own_sums = total(apart_near, F32)
    sums = jnp.broadcast_to(sums + own_sums, (Z_LO * X, 1, UNIT))
    sums = lax.all_to_all(sums, ("zlo", "x"), split_axis=0, concat_axis=0, tiled=True)
    return call(
        finish,
        [((ROWS, UNIT), F32)],
        [SMEM, SMEM, VMEM, VMEM, VMEM],
        (zhi[None], keep_mask, mine, other, sums),
    )[0]


def solution(mesh):
    physical = Mesh(
        mesh.devices.reshape(Z_LO, X, Y, Z_HI, CORE), ("zlo", "x", "y", "zhi", "core")
    )
    spec = P(("zlo", "x"), ("y", "zhi", "core"))
    return jax.shard_map(
        local, mesh=physical, in_specs=(spec, spec, spec), out_specs=spec, check_vma=False
    )
```

```python
import functools

import jax
import jax.numpy as jnp
from jax import lax
from jax.experimental import pallas as pl
from jax.experimental.pallas import tpu as pltpu
from jax.sharding import Mesh
from jax.sharding import PartitionSpec as P

Z_LO, X, Y, Z_HI, CORE = 4, 4, 8, 2, 2
ROWS, UNIT, TILE = 768, 384, 128
HALF = ROWS // 2
SUB = UNIT // (X * CORE)
WIDE = X * HALF
DEPTH = Y * Z_HI * CORE * SUB
VMEM = pl.BlockSpec(memory_space=pltpu.VMEM)
SMEM = pl.BlockSpec(memory_space=pltpu.SMEM)
HBM = pl.BlockSpec(memory_space=pltpu.HBM)
BF16, F32 = jnp.bfloat16, jnp.float32


def call(body, outs, ins, args, scratch=(), flops=0, vmem=48):
    shapes = [jax.ShapeDtypeStruct(shape, dtype) for shape, dtype in outs]
    moved = sum(a.size * a.dtype.itemsize for a in list(args) + shapes)
    return pl.pallas_call(
        body,
        out_shape=shapes,
        in_specs=ins,
        out_specs=[VMEM] * len(outs),
        scratch_shapes=scratch,
        compiler_params=pltpu.CompilerParams(vmem_limit_bytes=vmem << 20),
        cost_estimate=pl.CostEstimate(flops=flops, bytes_accessed=moved, transcendentals=0),
    )(*args)


def shift_y(shard, step):
    return lax.ppermute(shard, "y", [(i, (i + step) % Y) for i in range(Y)])


def shift_x(shard, step):
    return lax.ppermute(shard, "x", [(i, (i + step) % X) for i in range(X)])


def swap(shard, axis):
    return lax.ppermute(shard, axis, [(0, 1), (1, 0)])


def spread_over(array):
    return lax.all_to_all(array, ("x", "core"), split_axis=0, concat_axis=0, tiled=True)


def weigh(place, mask, values, both, far, weighted):
    zhi = place[0]
    for i in range(ROWS // TILE):
        for j in range(UNIT // TILE):
            at = (slice(i * TILE, (i + 1) * TILE), slice(j * TILE, (j + 1) * TILE))
            weighted[at] = values[at] * mask[i, j].astype(F32)
    for chunk in range(X * CORE):
        for part in range(CORE):
            start = part * UNIT + chunk * SUB
            both[chunk, 1 + part] = weighted[start : start + SUB].astype(BF16)
    near = weighted[pl.ds(pl.multiple_of(zhi * HALF, HALF), HALF)].T.astype(BF16)
    for chunk in range(X * CORE):
        both[chunk, 0] = near[chunk * SUB : (chunk + 1) * SUB]
    far[...] = weighted[pl.ds(pl.multiple_of((1 - zhi) * HALF, HALF), HALF)].T.astype(BF16)


def settle(place, both, near, right, stack):
    core = place[1]
    for x in range(X):
        for part in range(CORE):
            near[part * SUB : (part + 1) * SUB, x * HALF : (x + 1) * HALF] = both[x, part, 0]
    for own in range(2):
        source = core if own else 1 - core
        for x in range(X):
            for part in range(CORE):
                at = (x * CORE + part) * SUB
                stack[at : at + SUB] = both[x, source, 1 + part].astype(F32)
        right[0, own * UNIT : (own + 1) * UNIT] = stack[...].T.astype(BF16)


def multiply(order, place, *refs):
    shards, right = refs[: len(order)], refs[len(order)]
    outs, (a, b, sems) = refs[len(order) + 1 : -3], refs[-3:]
    y, zhi = place[0], place[1]
    copies = []
    for shard, (far, d, offset, length) in zip(shards, order):
        k_hi = 1 - zhi if far else zhi
        start = (lax.rem(y + Y - d, Y) * Z_HI + k_hi) * (CORE * SUB) + offset
        start = pl.multiple_of(start, SUB)
        copies.append(
            pltpu.make_async_copy(shard, a.at[pl.ds(start, length)], sems.at[len(copies)])
        )
    for own in range(2):
        for lo in range(Z_LO):
            origin = (zhi if own else 1 - zhi) * Z_LO + lo
            target = b.at[own, :, lo * UNIT : (lo + 1) * UNIT]
            copies.append(pltpu.make_async_copy(right.at[origin], target, sems.at[len(copies)]))
    for copy in copies:
        copy.start()
    for copy in copies[:-Z_LO]:
        copy.wait()
    step = 512
    for own in range(2):
        theirs, ours = outs[2 * own : 2 * own + 2]
        if own:
            for copy in copies[-Z_LO:]:
                copy.wait()

        @pl.loop(0, WIDE // step)
        def _(i):
            at = pl.ds(pl.multiple_of(i * step, step), step)
            product = jnp.dot(b[own], a[:, at], preferred_element_type=F32)
            theirs[:, at] = product[:UNIT].astype(BF16)
            ours[:, at] = product[UNIT:].astype(BF16)


def add_core(place, ours, sent, *pieces):
    for step in range(X):
        at = pl.ds(pl.multiple_of(lax.rem(place[0] + step, X) * HALF, HALF), HALF)
        pieces[step][...] = (ours[:, at].astype(F32) + sent[:, at].astype(F32)).astype(BF16)


def add_x(*refs):
    pieces, total, sums = refs[:X], refs[X], refs[X + 1]
    turned = sum(piece[...].astype(F32) for piece in pieces).T
    total[...] = turned.astype(total.dtype)
    sums[...] = jnp.sum(turned * turned, axis=0, keepdims=True)


def finish(place, keep, mine, other, sums, flows):
    zhi = place[0]
    scale = jnp.sum(sums[:, 0], axis=0, keepdims=True) / (ROWS * Z_LO * X) + 1e-06
    for own in range(2):
        base = (zhi if own else 1 - zhi) * (HALF // TILE)
        source = mine if own else other
        for i in range(HALF // TILE):
            rows = pl.ds(pl.multiple_of((base + i) * TILE, TILE), TILE)
            for j in range(UNIT // TILE):
                cols = slice(j * TILE, (j + 1) * TILE)
                value = source[i * TILE : (i + 1) * TILE, cols].astype(F32)
                kept = keep[base + i, j].astype(F32)
                flows[rows, cols] = kept * (value * value) / scale[:, cols]


def in_order(first, second):
    return lax.optimization_barrier((first, second))


def rings(near, far):
    shards, order = [near], [(0, 0, 0, CORE * SUB)]
    ends = [[near, near], [far, far]]
    for d in range(1, Y // 2):
        for which in (0, 1):
            up, down = ends[which]
            up, down = shift_y(up, 1), shift_y(down, -1)
            if d == 1 and which == 0:
                up, far = in_order(up, far)
                ends[1] = [far, far]
                shards.append(far)
                order.append((1, 0, 0, CORE * SUB))
            ends[which] = [up, down]
            shards += [up, down]
            order += [(which, d, 0, CORE * SUB), (which, Y - d, 0, CORE * SUB)]
    shards += [shift_y(ends[0][1], -1), shift_y(ends[1][0], 1)]
    order += [(0, Y // 2, 0, CORE * SUB), (1, Y // 2, 0, CORE * SUB)]
    return shards, tuple(order)


def local(values, tile_mask, keep_mask):
    x, y, core, zhi = (lax.axis_index(a) for a in ("x", "y", "core", "zhi"))
    place = jnp.stack([zhi, core])

    both, far = call(
        weigh,
        [((X * CORE, 3, SUB, UNIT), BF16), ((UNIT, HALF), BF16)],
        [SMEM, SMEM, VMEM],
        (place, tile_mask, values),
        [pltpu.VMEM((ROWS, UNIT), F32)],
    )
    far = swap(far, "zhi")
    both = spread_over(both)
    near, right = call(
        settle,
        [((CORE * SUB, WIDE), BF16), ((1, CORE * UNIT, UNIT), BF16)],
        [SMEM, VMEM],
        (place, both.reshape(X, CORE, 3, SUB, UNIT)),
        [pltpu.VMEM((UNIT, UNIT), F32)],
    )
    right, far = in_order(right, far)
    far = spread_over(far.reshape(X * CORE, SUB, HALF))
    right = lax.all_gather(right, ("zhi", "zlo"), axis=0, tiled=True)
    far = far.reshape(X, CORE * SUB, HALF).transpose(1, 0, 2).reshape(CORE * SUB, WIDE)
    shards, order = rings(near, far)

    theirs, ours, theirs_near, ours_near = call(
        functools.partial(multiply, order),
        [((UNIT, WIDE), BF16)] * 4,
        [SMEM] + [HBM] * (len(shards) + 1),
        (jnp.stack([y, zhi]), *shards, right),
        [
            pltpu.VMEM((DEPTH, WIDE), BF16),
            pltpu.VMEM((2, CORE * UNIT, DEPTH), BF16),
            pltpu.SemaphoreType.DMA((len(shards) + 2 * Z_LO,)),
        ],
        flops=4 * CORE * UNIT * DEPTH * WIDE,
        vmem=50,
    )

    def total(apart, dtype):
        return call(add_x, [((HALF, UNIT), dtype), ((1, UNIT), F32)], [VMEM] * X, apart)

    def over_x(ours, theirs):
        apart = call(
            add_core,
            [((UNIT, HALF), BF16)] * X,
            [SMEM, VMEM, VMEM],
            (x[None], ours, swap(theirs, "core")),
        )
        return [apart[0]] + [shift_x(apart[step], step) for step in range(1, X)]

    apart = over_x(ours, theirs)
    apart_near = over_x(ours_near, theirs_near)
    other, sums = total(apart, BF16)
    sums, other = in_order(swap(sums, "zhi"), other)
    other = swap(other, "zhi")
    mine, own_sums = total(apart_near, F32)
    sums = jnp.broadcast_to(sums + own_sums, (Z_LO * X, 1, UNIT))
    sums = lax.all_to_all(sums, ("zlo", "x"), split_axis=0, concat_axis=0, tiled=True)
    return call(
        finish,
        [((ROWS, UNIT), F32)],
        [SMEM, SMEM, VMEM, VMEM, VMEM],
        (zhi[None], keep_mask, mine, other, sums),
    )[0]


def solution(mesh):
    physical = Mesh(
        mesh.devices.reshape(Z_LO, X, Y, Z_HI, CORE), ("zlo", "x", "y", "zhi", "core")
    )
    spec = P(("zlo", "x"), ("y", "zhi", "core"))
    return jax.shard_map(
        local, mesh=physical, in_specs=(spec, spec, spec), out_specs=spec, check_vma=False
    )
```

```python
import functools

import jax
import jax.numpy as jnp
from jax import lax
from jax.experimental import pallas as pl
from jax.experimental.pallas import tpu as pltpu
from jax.sharding import Mesh
from jax.sharding import PartitionSpec as P

Z_LO, X, Y, Z_HI, CORE = 4, 4, 8, 2, 2
ROWS, UNIT, TILE = 768, 384, 128
HALF = ROWS // 2
SUB = UNIT // (X * CORE)
WIDE = X * HALF
DEPTH = Y * Z_HI * CORE * SUB
VMEM = pl.BlockSpec(memory_space=pltpu.VMEM)
SMEM = pl.BlockSpec(memory_space=pltpu.SMEM)
HBM = pl.BlockSpec(memory_space=pltpu.HBM)
BF16, F32 = jnp.bfloat16, jnp.float32


def call(body, outs, ins, args, scratch=(), flops=0, vmem=48):
    shapes = [jax.ShapeDtypeStruct(shape, dtype) for shape, dtype in outs]
    moved = sum(a.size * a.dtype.itemsize for a in list(args) + shapes)
    return pl.pallas_call(
        body,
        out_shape=shapes,
        in_specs=ins,
        out_specs=[VMEM] * len(outs),
        scratch_shapes=scratch,
        compiler_params=pltpu.CompilerParams(vmem_limit_bytes=vmem << 20),
        cost_estimate=pl.CostEstimate(flops=flops, bytes_accessed=moved, transcendentals=0),
    )(*args)


def shift_y(shard, step):
    return lax.ppermute(shard, "y", [(i, (i + step) % Y) for i in range(Y)])


def shift_x(shard, step):
    return lax.ppermute(shard, "x", [(i, (i + step) % X) for i in range(X)])


def swap(shard, axis):
    return lax.ppermute(shard, axis, [(0, 1), (1, 0)])


def spread_over(array):
    return lax.all_to_all(array, ("x", "core"), split_axis=0, concat_axis=0, tiled=True)


def weigh(place, mask, values, both, far, weighted):
    zhi = place[0]
    for i in range(ROWS // TILE):
        for j in range(UNIT // TILE):
            at = (slice(i * TILE, (i + 1) * TILE), slice(j * TILE, (j + 1) * TILE))
            weighted[at] = values[at] * mask[i, j].astype(F32)
    for chunk in range(X * CORE):
        for part in range(CORE):
            start = part * UNIT + chunk * SUB
            both[chunk, 1 + part] = weighted[start : start + SUB].astype(BF16)
    near = weighted[pl.ds(pl.multiple_of(zhi * HALF, HALF), HALF)].T.astype(BF16)
    for chunk in range(X * CORE):
        both[chunk, 0] = near[chunk * SUB : (chunk + 1) * SUB]
    far[...] = weighted[pl.ds(pl.multiple_of((1 - zhi) * HALF, HALF), HALF)].T.astype(BF16)


def settle(place, both, near, right, stack):
    core = place[1]
    for x in range(X):
        for part in range(CORE):
            near[part * SUB : (part + 1) * SUB, x * HALF : (x + 1) * HALF] = both[x, part, 0]
    for own in range(2):
        source = core if own else 1 - core
        for x in range(X):
            for part in range(CORE):
                at = (x * CORE + part) * SUB
                stack[at : at + SUB] = both[x, source, 1 + part].astype(F32)
        right[0, own * UNIT : (own + 1) * UNIT] = stack[...].T.astype(BF16)


def multiply(order, place, *refs):
    shards, right = refs[: len(order)], refs[len(order)]
    outs, (a, b, sems) = refs[len(order) + 1 : -3], refs[-3:]
    y, zhi = place[0], place[1]
    copies = []
    for shard, (far, d, offset, length) in zip(shards, order):
        k_hi = 1 - zhi if far else zhi
        start = (lax.rem(y + Y - d, Y) * Z_HI + k_hi) * (CORE * SUB) + offset
        start = pl.multiple_of(start, SUB)
        copies.append(
            pltpu.make_async_copy(shard, a.at[pl.ds(start, length)], sems.at[len(copies)])
        )
    for own in range(2):
        for lo in range(Z_LO):
            origin = (zhi if own else 1 - zhi) * Z_LO + lo
            target = b.at[own, :, lo * UNIT : (lo + 1) * UNIT]
            copies.append(pltpu.make_async_copy(right.at[origin], target, sems.at[len(copies)]))
    for copy in copies:
        copy.start()
    for copy in copies[:-Z_LO]:
        copy.wait()
    step = 512
    for own in range(2):
        theirs, ours = outs[2 * own : 2 * own + 2]
        if own:
            for copy in copies[-Z_LO:]:
                copy.wait()
        for start in range(0, WIDE, step):
            at = slice(start, start + step)
            product = jnp.dot(b[own], a[:, at], preferred_element_type=F32)
            theirs[:, at] = product[:UNIT].astype(BF16)
            ours[:, at] = product[UNIT:].astype(BF16)


def add_core(place, ours, sent, *pieces):
    for step in range(X):
        at = pl.ds(pl.multiple_of(lax.rem(place[0] + step, X) * HALF, HALF), HALF)
        pieces[step][...] = (ours[:, at].astype(F32) + sent[:, at].astype(F32)).astype(BF16)


def add_x(*refs):
    pieces, total, sums = refs[:X], refs[X], refs[X + 1]
    turned = sum(piece[...].astype(F32) for piece in pieces).T
    total[...] = turned.astype(total.dtype)
    sums[...] = jnp.sum(turned * turned, axis=0, keepdims=True)


def finish(place, keep, mine, other, sums, flows):
    zhi = place[0]
    scale = jnp.sum(sums[:, 0], axis=0, keepdims=True) / (ROWS * Z_LO * X) + 1e-06
    for own in range(2):
        base = (zhi if own else 1 - zhi) * (HALF // TILE)
        source = mine if own else other
        for i in range(HALF // TILE):
            rows = pl.ds(pl.multiple_of((base + i) * TILE, TILE), TILE)
            for j in range(UNIT // TILE):
                cols = slice(j * TILE, (j + 1) * TILE)
                value = source[i * TILE : (i + 1) * TILE, cols].astype(F32)
                kept = keep[base + i, j].astype(F32)
                flows[rows, cols] = kept * (value * value) / scale[:, cols]


def in_order(first, second):
    return lax.optimization_barrier((first, second))


def rings(near, far):
    shards, order = [near], [(0, 0, 0, CORE * SUB)]
    ends = [[near, near], [far, far]]
    for d in range(1, Y // 2):
        for which in (0, 1):
            up, down = ends[which]
            up, down = shift_y(up, 1), shift_y(down, -1)
            if d == 1 and which == 0:
                up, far = in_order(up, far)
                ends[1] = [far, far]
                shards.append(far)
                order.append((1, 0, 0, CORE * SUB))
            ends[which] = [up, down]
            shards += [up, down]
            order += [(which, d, 0, CORE * SUB), (which, Y - d, 0, CORE * SUB)]
    shards += [shift_y(ends[0][1], -1), shift_y(ends[1][0], 1)]
    order += [(0, Y // 2, 0, CORE * SUB), (1, Y // 2, 0, CORE * SUB)]
    return shards, tuple(order)


def local(values, tile_mask, keep_mask):
    x, y, core, zhi = (lax.axis_index(a) for a in ("x", "y", "core", "zhi"))
    place = jnp.stack([zhi, core])

    both, far = call(
        weigh,
        [((X * CORE, 3, SUB, UNIT), BF16), ((UNIT, HALF), BF16)],
        [SMEM, SMEM, VMEM],
        (place, tile_mask, values),
        [pltpu.VMEM((ROWS, UNIT), F32)],
    )
    far = swap(far, "zhi")
    both = spread_over(both)
    near, right = call(
        settle,
        [((CORE * SUB, WIDE), BF16), ((1, CORE * UNIT, UNIT), BF16)],
        [SMEM, VMEM],
        (place, both.reshape(X, CORE, 3, SUB, UNIT)),
        [pltpu.VMEM((UNIT, UNIT), F32)],
    )
    right, far = in_order(right, far)
    far = spread_over(far.reshape(X * CORE, SUB, HALF))
    right = lax.all_gather(right, ("zhi", "zlo"), axis=0, tiled=True)
    far = far.reshape(X, CORE * SUB, HALF).transpose(1, 0, 2).reshape(CORE * SUB, WIDE)
    shards, order = rings(near, far)

    theirs, ours, theirs_near, ours_near = call(
        functools.partial(multiply, order),
        [((UNIT, WIDE), BF16)] * 4,
        [SMEM] + [HBM] * (len(shards) + 1),
        (jnp.stack([y, zhi]), *shards, right),
        [
            pltpu.VMEM((DEPTH, WIDE), BF16),
            pltpu.VMEM((2, CORE * UNIT, DEPTH), BF16),
            pltpu.SemaphoreType.DMA((len(shards) + 2 * Z_LO,)),
        ],
        flops=4 * CORE * UNIT * DEPTH * WIDE,
        vmem=50,
    )

    def total(apart, dtype):
        return call(add_x, [((HALF, UNIT), dtype), ((1, UNIT), F32)], [VMEM] * X, apart)

    def over_x(ours, theirs):
        apart = call(
            add_core,
            [((UNIT, HALF), BF16)] * X,
            [SMEM, VMEM, VMEM],
            (x[None], ours, swap(theirs, "core")),
        )
        return [apart[0]] + [shift_x(apart[step], step) for step in range(1, X)]

    apart = over_x(ours, theirs)
    apart_near = over_x(ours_near, theirs_near)
    other, sums = total(apart, BF16)
    sums, other = in_order(swap(sums, "zhi"), other)
    other = swap(other, "zhi")
    mine, own_sums = total(apart_near, F32)
    sums = jnp.broadcast_to(sums + own_sums, (Z_LO * X, 1, UNIT))
    sums = lax.all_to_all(sums, ("zlo", "x"), split_axis=0, concat_axis=0, tiled=True)
    return call(
        finish,
        [((ROWS, UNIT), F32)],
        [SMEM, SMEM, VMEM, VMEM, VMEM],
        (zhi[None], keep_mask, mine, other, sums),
    )[0]


def solution(mesh):
    physical = Mesh(
        mesh.devices.reshape(Z_LO, X, Y, Z_HI, CORE), ("zlo", "x", "y", "zhi", "core")
    )
    spec = P(("zlo", "x"), ("y", "zhi", "core"))
    return jax.shard_map(
        local, mesh=physical, in_specs=(spec, spec, spec), out_specs=spec, check_vma=False
    )
```

```python
import functools

import jax
import jax.numpy as jnp
from jax import lax
from jax.experimental import pallas as pl
from jax.experimental.pallas import tpu as pltpu
from jax.sharding import Mesh
from jax.sharding import PartitionSpec as P

Z_LO, X, Y, Z_HI, CORE = 4, 4, 8, 2, 2
ROWS, UNIT, TILE = 768, 384, 128
HALF = ROWS // 2
SUB = UNIT // (X * CORE)
WIDE = X * HALF
DEPTH = Y * Z_HI * CORE * SUB
VMEM = pl.BlockSpec(memory_space=pltpu.VMEM)
SMEM = pl.BlockSpec(memory_space=pltpu.SMEM)
HBM = pl.BlockSpec(memory_space=pltpu.HBM)
BF16, F32 = jnp.bfloat16, jnp.float32


def call(body, outs, ins, args, scratch=(), flops=0, vmem=48):
    shapes = [jax.ShapeDtypeStruct(shape, dtype) for shape, dtype in outs]
    moved = sum(a.size * a.dtype.itemsize for a in list(args) + shapes)
    return pl.pallas_call(
        body,
        out_shape=shapes,
        in_specs=ins,
        out_specs=[VMEM] * len(outs),
        scratch_shapes=scratch,
        compiler_params=pltpu.CompilerParams(vmem_limit_bytes=vmem << 20),
        cost_estimate=pl.CostEstimate(flops=flops, bytes_accessed=moved, transcendentals=0),
    )(*args)


def shift_y(shard, step):
    return lax.ppermute(shard, "y", [(i, (i + step) % Y) for i in range(Y)])


def shift_x(shard, step):
    return lax.ppermute(shard, "x", [(i, (i + step) % X) for i in range(X)])


def swap(shard, axis):
    return lax.ppermute(shard, axis, [(0, 1), (1, 0)])


def spread_over(array):
    return lax.all_to_all(array, ("x", "core"), split_axis=0, concat_axis=0, tiled=True)


def weigh(place, mask, values, both, far, weighted):
    zhi = place[0]
    for i in range(ROWS // TILE):
        for j in range(UNIT // TILE):
            at = (slice(i * TILE, (i + 1) * TILE), slice(j * TILE, (j + 1) * TILE))
            weighted[at] = values[at] * mask[i, j].astype(F32)
    for chunk in range(X * CORE):
        for part in range(CORE):
            start = part * UNIT + chunk * SUB
            both[chunk, 1 + part] = weighted[start : start + SUB].astype(BF16)
    near = weighted[pl.ds(pl.multiple_of(zhi * HALF, HALF), HALF)].T.astype(BF16)
    for chunk in range(X * CORE):
        both[chunk, 0] = near[chunk * SUB : (chunk + 1) * SUB]
    far[...] = weighted[pl.ds(pl.multiple_of((1 - zhi) * HALF, HALF), HALF)].T.astype(BF16)


def settle(place, both, near, right, stack):
    core = place[1]
    for x in range(X):
        for part in range(CORE):
            near[part * SUB : (part + 1) * SUB, x * HALF : (x + 1) * HALF] = both[x, part, 0]
    for own in range(2):
        source = core if own else 1 - core
        for x in range(X):
            for part in range(CORE):
                at = (x * CORE + part) * SUB
                stack[at : at + SUB] = both[x, source, 1 + part].astype(F32)
        right[0, own * UNIT : (own + 1) * UNIT] = stack[...].T.astype(BF16)


def multiply(order, place, *refs):
    shards, right = refs[: len(order)], refs[len(order)]
    outs, (a, b, sems) = refs[len(order) + 1 : -3], refs[-3:]
    y, zhi = place[0], place[1]
    copies = []
    for shard, (far, d, offset, length) in zip(shards, order):
        k_hi = 1 - zhi if far else zhi
        start = (lax.rem(y + Y - d, Y) * Z_HI + k_hi) * (CORE * SUB) + offset
        start = pl.multiple_of(start, SUB)
        copies.append(
            pltpu.make_async_copy(shard, a.at[pl.ds(start, length)], sems.at[len(copies)])
        )
    for own in range(2):
        for lo in range(Z_LO):
            origin = (zhi if own else 1 - zhi) * Z_LO + lo
            target = b.at[own, :, lo * UNIT : (lo + 1) * UNIT]
            copies.append(pltpu.make_async_copy(right.at[origin], target, sems.at[len(copies)]))
    for copy in copies:
        copy.start()
    for copy in copies[:-Z_LO]:
        copy.wait()
    step = 512
    for own in range(2):
        theirs, ours = outs[2 * own : 2 * own + 2]
        if own:
            for copy in copies[-Z_LO:]:
                copy.wait()
        for start in range(0, WIDE, step):
            at = slice(start, start + step)
            product = jnp.dot(b[own], a[:, at], preferred_element_type=F32)
            theirs[:, at] = product[:UNIT].astype(BF16)
            ours[:, at] = product[UNIT:].astype(BF16)


def add_core(place, ours, sent, *pieces):
    for step in range(X):
        at = pl.ds(pl.multiple_of(lax.rem(place[0] + step, X) * HALF, HALF), HALF)
        pieces[step][...] = (ours[:, at].astype(F32) + sent[:, at].astype(F32)).astype(BF16)


def add_x(*refs):
    pieces, total, sums = refs[:X], refs[X], refs[X + 1]
    turned = sum(piece[...].astype(F32) for piece in pieces).T
    total[...] = turned.astype(total.dtype)
    sums[...] = jnp.sum(turned * turned, axis=0, keepdims=True)


def add_x_last(*refs):
    pieces, earlier, total, sums = refs[:X], refs[X], refs[X + 1], refs[X + 2]
    turned = sum(piece[...].astype(F32) for piece in pieces).T
    total[...] = turned
    both = jnp.sum(turned * turned, axis=0, keepdims=True) + earlier[...]
    sums[...] = jnp.broadcast_to(both[None], sums.shape)


def finish(place, keep, mine, other, sums, flows):
    zhi = place[0]
    scale = jnp.sum(sums[:, 0], axis=0, keepdims=True) / (ROWS * Z_LO * X) + 1e-06
    for own in range(2):
        base = (zhi if own else 1 - zhi) * (HALF // TILE)
        source = mine if own else other
        for i in range(HALF // TILE):
            rows = pl.ds(pl.multiple_of((base + i) * TILE, TILE), TILE)
            for j in range(UNIT // TILE):
                cols = slice(j * TILE, (j + 1) * TILE)
                value = source[i * TILE : (i + 1) * TILE, cols].astype(F32)
                kept = keep[base + i, j].astype(F32)
                flows[rows, cols] = kept * (value * value) / scale[:, cols]


def in_order(first, second):
    return lax.optimization_barrier((first, second))


def rings(near, far):
    shards, order = [near], [(0, 0, 0, CORE * SUB)]
    ends = [[near, near], [far, far]]
    for d in range(1, Y // 2):
        for which in (0, 1):
            up, down = ends[which]
            up, down = shift_y(up, 1), shift_y(down, -1)
            if d == 1 and which == 0:
                up, far = in_order(up, far)
                ends[1] = [far, far]
                shards.append(far)
                order.append((1, 0, 0, CORE * SUB))
            ends[which] = [up, down]
            shards += [up, down]
            order += [(which, d, 0, CORE * SUB), (which, Y - d, 0, CORE * SUB)]
    shards += [shift_y(ends[0][1], -1), shift_y(ends[1][0], 1)]
    order += [(0, Y // 2, 0, CORE * SUB), (1, Y // 2, 0, CORE * SUB)]
    return shards, tuple(order)


def local(values, tile_mask, keep_mask):
    x, y, core, zhi = (lax.axis_index(a) for a in ("x", "y", "core", "zhi"))
    place = jnp.stack([zhi, core])

    both, far = call(
        weigh,
        [((X * CORE, 3, SUB, UNIT), BF16), ((UNIT, HALF), BF16)],
        [SMEM, SMEM, VMEM],
        (place, tile_mask, values),
        [pltpu.VMEM((ROWS, UNIT), F32)],
    )
    far = swap(far, "zhi")
    both = spread_over(both)
    near, right = call(
        settle,
        [((CORE * SUB, WIDE), BF16), ((1, CORE * UNIT, UNIT), BF16)],
        [SMEM, VMEM],
        (place, both.reshape(X, CORE, 3, SUB, UNIT)),
        [pltpu.VMEM((UNIT, UNIT), F32)],
    )
    right, far = in_order(right, far)
    far = spread_over(far.reshape(X * CORE, SUB, HALF))
    right = lax.all_gather(right, ("zhi", "zlo"), axis=0, tiled=True)
    far = far.reshape(X, CORE * SUB, HALF).transpose(1, 0, 2).reshape(CORE * SUB, WIDE)
    shards, order = rings(near, far)

    theirs, ours, theirs_near, ours_near = call(
        functools.partial(multiply, order),
        [((UNIT, WIDE), BF16)] * 4,
        [SMEM] + [HBM] * (len(shards) + 1),
        (jnp.stack([y, zhi]), *shards, right),
        [
            pltpu.VMEM((DEPTH, WIDE), BF16),
            pltpu.VMEM((2, CORE * UNIT, DEPTH), BF16),
            pltpu.SemaphoreType.DMA((len(shards) + 2 * Z_LO,)),
        ],
        flops=4 * CORE * UNIT * DEPTH * WIDE,
        vmem=50,
    )

    def total(apart, dtype):
        return call(add_x, [((HALF, UNIT), dtype), ((1, UNIT), F32)], [VMEM] * X, apart)

    def over_x(ours, theirs):
        apart = call(
            add_core,
            [((UNIT, HALF), BF16)] * X,
            [SMEM, VMEM, VMEM],
            (x[None], ours, swap(theirs, "core")),
        )
        return [apart[0]] + [shift_x(apart[step], step) for step in range(1, X)]

    apart = over_x(ours, theirs)
    apart_near = over_x(ours_near, theirs_near)
    other, sums = total(apart, BF16)
    sums, other = in_order(swap(sums, "zhi"), other)
    other = swap(other, "zhi")
    mine, sums = call(
        add_x_last,
        [((HALF, UNIT), F32), ((Z_LO * X, 1, UNIT), F32)],
        [VMEM] * (X + 1),
        (*apart_near, sums),
    )
    sums = lax.all_to_all(sums, ("zlo", "x"), split_axis=0, concat_axis=0, tiled=True)
    return call(
        finish,
        [((ROWS, UNIT), F32)],
        [SMEM, SMEM, VMEM, VMEM, VMEM],
        (zhi[None], keep_mask, mine, other, sums),
    )[0]


def solution(mesh):
    physical = Mesh(
        mesh.devices.reshape(Z_LO, X, Y, Z_HI, CORE), ("zlo", "x", "y", "zhi", "core")
    )
    spec = P(("zlo", "x"), ("y", "zhi", "core"))
    return jax.shard_map(
        local, mesh=physical, in_specs=(spec, spec, spec), out_specs=spec, check_vma=False
    )
```
